128 devices in a mesh: sp: 16 (over z, y), tp: 8 (over x, core).
Axes of the slice: x: 4, y: 4, z: 4, core: 2. Of those that a mesh axis runs over, the one named last changes fastest.
Arguments:
- tokens: bfloat16 [8192, 5120], P('sp', 'tp'), may hold values from -6 to 6
- w_query: bfloat16 [5120, 5120], P(None, 'tp'), may hold values from -0.078125 to 0.078125
- w_key: bfloat16 [5120, 5120], P(None, 'tp'), may hold values from -0.078125 to 0.078125
- w_value: bfloat16 [5120, 5120], P(None, 'tp'), may hold values from -0.078125 to 0.078125
- cache_keys: bfloat16 [64, 128, 5120], P('sp', None, 'tp'), may hold values from -256 to 256, as said below
- cache_values: bfloat16 [64, 128, 5120], P('sp', None, 'tp'), may hold values from -6 to 6
- tile_level: int32 [64], P('sp'), may hold values from 0 to 2
- window_map: int32 [16, 8], replicated, may hold values from 0 to 63, as said below
Outputs:
- attended: bfloat16 [8192, 5120], P('sp', 'tp')
The draws below stay inside these ranges and needn't reach their ends.
Inputs may be any that keep to these rules, and one draw needn't show every extreme that they name: `window_map`: row d lists 8 blocks held by 8 different indices of sp, one block from each; block b is held by index b // 4. `cache_keys`: cached keys mostly of order one.
All inputs are finite; a program needn't handle non-finite values.
Results may differ from the reference program's by a relative error of at most 0.0079.
Values may be sent and summed in bfloat16 or wider, within the bound.
A program may use at most 128 MiB of HBM per device.

```python
import math
import jax
import jax.numpy as jnp
from jax import lax

D = 5120
HEADS = 40
HD = 128
TOK_DEV = 512
TILE = 128
BLOCK = 128
BLK_DEV = 4
TOKENS = 8192
TILES = 64
NBLK = 64
WIN = 8
N_SP = 16


def draw_cache_keys(key, part):
    key = jax.random.fold_in(key, 11)
    shape = (BLK_DEV * N_SP, BLOCK, D)
    drawn = jnp.clip(jax.random.normal(key, shape, jnp.float32), -6.0, 6.0)
    return drawn.astype(jnp.bfloat16)


def draw_window_map(key, part):
    key = jax.random.fold_in(key, 5)
    slots = jnp.arange(N_SP // 2, dtype=jnp.int32)

    def one_owner(owner_index):
        owner_key = jax.random.fold_in(key, owner_index)
        holder_key, local_key, middle_key = jax.random.split(owner_key, 3)
        holders = jax.random.permutation(holder_key, jnp.arange(N_SP, dtype=jnp.int32))[:N_SP // 2]
        local_index = jax.random.randint(local_key, (N_SP // 2,), 0, BLK_DEV).astype(jnp.int32)
        middle = 1 + jax.random.permutation(middle_key, jnp.arange(N_SP - 2, dtype=jnp.int32))[:N_SP // 2 - 2]
        edge_holders = jnp.concatenate([jnp.zeros((1,), jnp.int32), jnp.full((1,), N_SP - 1, jnp.int32), middle.astype(jnp.int32)])
        edge_local = jnp.where(slots == 0, 0, jnp.where(slots == 1, BLK_DEV - 1, local_index)).astype(jnp.int32)
        first_row = owner_index == 0
        chosen_holders = jnp.where(first_row, edge_holders, holders)
        chosen_local = jnp.where(first_row, edge_local, local_index)
        return (chosen_holders * BLK_DEV + chosen_local).astype(jnp.int32)
    return jax.vmap(one_owner)(jnp.arange(N_SP, dtype=jnp.int32))


def with_ends(result, own_key, low, high):
    index_at = [jax.random.randint(jax.random.fold_in(own_key, axis), (), 0, length) for axis, length in enumerate(result.shape)]
    widest = result.shape.index(max(result.shape))
    next_to = index_at[:widest] + [(index_at[widest] + 1) % result.shape[widest]] + index_at[widest + 1:]
    return result.at[tuple(index_at)].set(low).at[tuple(next_to)].set(high)


def shard_levels(rng, shape, cuts, smallest, high):
    def one(axis_at, parts):
        steps = jax.random.uniform(jax.random.fold_in(jax.random.fold_in(rng, 6), axis_at), (parts,), jnp.float32, smallest / len(cuts), high / len(cuts))
        return jnp.repeat(jnp.exp(steps), shape[axis_at] // parts).reshape((-1,) + (1,) * (len(shape) - axis_at - 1))

    level = one(*cuts[0])
    for cut in cuts[1:]:
        level = level * one(*cut)
    return level


def gaussian(own_key, shape, width, bound, pieces=(), kind=jnp.bfloat16):
    result = width * jax.random.normal(own_key, shape, jnp.float32)
    if pieces:
        result = result * shard_levels(own_key, shape, pieces, -0.22, 0.18)
    return jnp.clip(result, -bound, bound).astype(kind)


def setup_inputs(seed: int = 0) -> dict:
    splits = jax.random.split(jax.random.key(seed), 9)
    tokens = gaussian(splits[0], (TOKENS, D), 1.0, 6.0, ((0, 16), (1, 8)))
    w_query = gaussian(splits[1], (D, D), D ** -0.5, 0.078125, ((1, 8),))
    w_key = gaussian(splits[2], (D, D), D ** -0.5, 0.078125, ((1, 8),))
    w_value = gaussian(splits[3], (D, D), D ** -0.5, 0.078125, ((1, 8),))
    cache_keys = draw_cache_keys(jax.random.fold_in(splits[8], 71), 0)
    cache_values = gaussian(splits[5], (NBLK, BLOCK, D), 1.0, 6.0, ((0, 16), (2, 8)))
    tile_level = with_ends(jax.random.randint(splits[6], (TILES,), 0, 3), jax.random.fold_in(splits[6], 1), 0, 2).astype(jnp.int32)
    window_map = draw_window_map(jax.random.fold_in(splits[8], 71), 0)
    return dict(tokens=tokens, w_query=w_query, w_key=w_key, w_value=w_value, cache_keys=cache_keys, cache_values=cache_values, tile_level=tile_level, window_map=window_map)


def reference(tokens, w_query, w_key, w_value, cache_keys, cache_values, tile_level, window_map):
    queries = jnp.dot(tokens, w_query, preferred_element_type=jnp.float32).astype(jnp.bfloat16)
    keys_all = jnp.dot(tokens, w_key, preferred_element_type=jnp.float32).astype(jnp.bfloat16)
    values_all = jnp.dot(tokens, w_value, preferred_element_type=jnp.float32).astype(jnp.bfloat16)
    padding = jnp.zeros((TOK_DEV, D), jnp.bfloat16)
    keys_padded = jnp.concatenate([padding, keys_all, padding], axis=0)
    values_padded = jnp.concatenate([padding, values_all, padding], axis=0)
    token_levels = jnp.repeat(tile_level, TILE)
    score_scale = 1.0 / math.sqrt(HD)

    def per_owner(owner_index):
        start = owner_index * TOK_DEV
        own_queries = lax.dynamic_slice_in_dim(queries, start, TOK_DEV, 0)
        band_keys = lax.dynamic_slice_in_dim(keys_padded, start, 3 * TOK_DEV, 0)
        band_values = lax.dynamic_slice_in_dim(values_padded, start, 3 * TOK_DEV, 0)
        own_levels = lax.dynamic_slice_in_dim(token_levels, start, TOK_DEV, 0)
        radius = (own_levels + 1) * TOK_DEV // 3
        query_pos = start + jnp.arange(TOK_DEV, dtype=jnp.int32)
        key_pos = start - TOK_DEV + jnp.arange(3 * TOK_DEV, dtype=jnp.int32)
        distance = jnp.abs(key_pos[None, :] - query_pos[:, None])
        allowed = (distance <= radius[:, None]) & (key_pos[None, :] >= 0) & (key_pos[None, :] < TOKENS)
        blocks = lax.dynamic_index_in_dim(window_map, owner_index, 0, keepdims=False)
        fetched_keys = jnp.take(cache_keys, blocks, axis=0).reshape(WIN * BLOCK, D)
        fetched_values = jnp.take(cache_values, blocks, axis=0).reshape(WIN * BLOCK, D)
        all_keys = jnp.concatenate([fetched_keys, band_keys], axis=0)
        all_values = jnp.concatenate([fetched_values, band_values], axis=0)
        allowed_all = jnp.concatenate([jnp.ones((TOK_DEV, WIN * BLOCK), bool), allowed], axis=1)
        query_heads = own_queries.reshape(TOK_DEV, HEADS, HD).astype(jnp.float32)
        key_heads = all_keys.reshape(-1, HEADS, HD).astype(jnp.float32)
        value_heads = all_values.reshape(-1, HEADS, HD).astype(jnp.float32)
        scores = jnp.einsum('qhe,khe->hqk', query_heads, key_heads) * score_scale
        scores = jnp.where(allowed_all[None], scores, -jnp.inf)
        largest = lax.optimization_barrier(jnp.max(scores, axis=2, keepdims=True))
        weights = jnp.exp(scores - largest)
        total = lax.optimization_barrier(jnp.sum(weights, axis=2, keepdims=True))
        rounded = lax.optimization_barrier(weights.astype(jnp.bfloat16)).astype(jnp.float32)
        mixed = jnp.einsum('hqk,khe->hqe', rounded, value_heads) / total
        return mixed.transpose(1, 0, 2).reshape(TOK_DEV, D).astype(jnp.bfloat16)
    results = lax.map(per_owner, jnp.arange(N_SP, dtype=jnp.int32))
    return results.reshape(TOKENS, D)
```

```python
import functools
import math

import jax
import jax.numpy as jnp
from jax import lax
from jax.experimental import pallas as pl
from jax.experimental.pallas import tpu as pltpu
from jax.sharding import PartitionSpec as P

HD = 128
TILE = 128
BLOCK = 128
MESH = pl.DeviceIdType.MESH
LOW = -1e30
SCALE = math.log2(math.e) / math.sqrt(HD)
ROUNDS = ((0, 1), (1, 2), (3, 1))
COLUMN = (0, 1, 3, 2)


def kernel(
    tokens, w_query, w_key, w_value, cache_keys, cache_values, tile_level, window_map,
    out,
    tok, weights, total, q_buf, kv_own, halo, held_0, held_1, held_2, held_3, send, row, passing, m_buf, l_buf, acc_buf,
    weight_sem, local_sem, send_sem, recv_sem,
):
    sp = lax.axis_index("sp")
    tp = lax.axis_index("tp")
    z, y = sp // 4, sp % 4
    x, core = tp // 2, tp % 2
    rows, width = tokens.shape
    heads = width // HD

    sibling = (sp, x * 2 + 1 - core)
    x_up = (sp, ((x + 1) % 4) * 2 + core)
    x_down = (sp, ((x + 3) % 4) * 2 + core)
    y_up = (z * 4 + (y + 1) % 4, tp)
    y_down = (z * 4 + (y + 3) % 4, tp)
    z_up = (((z + 1) % 4) * 4 + y, tp)
    z_down = (((z + 3) % 4) * 4 + y, tp)
    after = ((sp + 1) % 16, tp)
    before = ((sp + 15) % 16, tp)
    gathered = (held_0, held_1, held_2, held_3)
    peers = (sibling, x_up, x_down, y_up, y_down, z_up, z_down, after, before)

    barrier = pltpu.get_barrier_semaphore()
    for peer in peers:
        pl.semaphore_signal(barrier, inc=1, device_id=peer, device_id_type=MESH)

    lane = pl.ds(pl.multiple_of(core * width, HD), width)
    own_tokens = pltpu.make_async_copy(tokens, tok.at[0, :, lane], local_sem.at[0])
    own_keys = pltpu.make_async_copy(cache_keys, gathered[0].at[0], local_sem.at[1])
    own_values = pltpu.make_async_copy(cache_values, gathered[0].at[1], local_sem.at[2])
    own_keys.start()
    own_values.start()
    own_tokens.start()
    depth = 2 * width
    weight_copies = {}
    for back in (0, 1, 3, 2):
        source = pl.ds(pl.multiple_of(((x + 4 - back) % 4) * depth, depth), depth)
        for j, w in enumerate((w_query, w_key, w_value)):
            copy = pltpu.make_async_copy(
                w.at[source, :], weights.at[back, :, pl.ds(j * width, width)], weight_sem.at[back, j]
            )
            copy.start()
            weight_copies[back, j] = copy

    pl.semaphore_wait(barrier, len(peers))

    copies = []

    def remote(src, dst, peer):
        at = len(copies)
        copy = pltpu.make_async_remote_copy(
            src_ref=src, dst_ref=dst, send_sem=send_sem.at[at], recv_sem=recv_sem.at[at],
            device_id=peer, device_id_type=MESH,
        )
        copy.start()
        copies.append(copy)
        return copy

    to_sibling = [remote(tokens, tok.at[0, :, lane], sibling)]
    y_first = []
    for kv, cache in enumerate((cache_keys, cache_values)):
        y_first.append(remote(cache, gathered[1].at[kv], y_up))
        y_first.append(remote(cache, gathered[3].at[kv], y_down))
    x_from_down = remote(tokens, tok.at[1, :, lane], x_up)
    x_from_up = remote(tokens, tok.at[3, :, lane], x_down)

    def wanted(holder, owner):
        local, found = jnp.int32(0), jnp.int32(0)
        for k in range(8):
            block = window_map[owner, k]
            hit = jnp.where(block // 4 == holder, 1, 0)
            local = local + hit * (block % 4)
            found = found + hit
        return local, found

    def pick(position):
        column = COLUMN[position]
        holder = z * 4 + (y + 4 - column) % 4
        for step, owner_z in ((0, z), (1, (z + 1) % 4), (2, (z + 2) % 4), (3, (z + 3) % 4)):
            local, _ = wanted(holder, owner_z * 4 + y)
            for kv in range(2):
                block = gathered[column][kv, local]
                if step == 0:
                    row[kv, 0, position] = block
                else:
                    send[kv, step - 1, position] = block

    z_copies = {}

    def z_send(number):
        first, count = ROUNDS[number]
        slots = pl.ds(first, count)
        far_keys = remote(send.at[0, 1, slots], passing.at[0, slots], z_up)
        far_values = remote(send.at[1, 1, slots], passing.at[1, slots], z_down)
        near = []
        for kv in range(2):
            near.append(remote(send.at[kv, 0, slots], row.at[kv, 1, slots], z_up))
            near.append(remote(send.at[kv, 2, slots], row.at[kv, 3, slots], z_down))
        z_copies[number] = (far_keys, far_values, near)

    z_far = {}

    def z_pass(number):
        first, count = ROUNDS[number]
        slots = pl.ds(first, count)
        far_keys, far_values, _ = z_copies[number]
        far_keys.wait_recv()
        a = remote(passing.at[0, slots], row.at[0, 2, slots], z_up)
        far_values.wait_recv()
        b = remote(passing.at[1, slots], row.at[1, 2, slots], z_down)
        z_far[number] = (a, b)

    def project(back, start):
        for j in range(3):
            weight_copies[back, j].wait()

        @pl.loop(0, 3)
        def _(j):
            columns = pl.ds(pl.multiple_of(j * width, HD), width)
            product = jnp.dot(tok[back], weights[back, :, columns], preferred_element_type=jnp.float32)
            if start:
                total[:, columns] = product
            else:
                total[:, columns] += product

    own_keys.wait()
    own_values.wait()
    pick(0)
    z_send(0)

    own_tokens.wait()
    to_sibling[0].wait_recv()
    project(0, True)
    z_pass(0)

    half = rows // 2
    x_from_down.wait_recv()
    x_far = [remote(tok.at[1, pl.ds(0, half), lane], tok.at[2, pl.ds(0, half), lane], x_up)]
    x_from_up.wait_recv()
    x_far.append(remote(tok.at[3, pl.ds(half, half), lane], tok.at[2, pl.ds(half, half), lane], x_down))
    sibling_down = remote(tok.at[1, :, lane], tok.at[1, :, lane], sibling)
    sibling_up = remote(tok.at[3, :, lane], tok.at[3, :, lane], sibling)
    sibling_down.wait_recv()
    project(1, False)
    sibling_up.wait_recv()
    project(3, False)
    sibling_far = []
    for part in range(2):
        piece = pl.ds(part * half, half)
        x_far[part].wait_recv()
        sibling_far.append(remote(tok.at[2, piece, lane], tok.at[2, piece, lane], sibling))
    for copy in sibling_far:
        copy.wait_recv()
    project(2, False)

    @pl.loop(0, heads)
    def _(h):
        q_buf[h] = total[:, pl.ds(pl.multiple_of(h * HD, HD), HD)].astype(jnp.bfloat16)

    kv_own[0] = total[:, width : 2 * width].astype(jnp.bfloat16)
    kv_own[1] = total[:, 2 * width : 3 * width].astype(jnp.bfloat16)

    for copy in y_first:
        copy.wait_recv()
    y_far = []
    for kv in range(2):
        low, high = pl.ds(0, 2), pl.ds(2, 2)
        y_far.append(remote(gathered[1].at[kv, low], gathered[2].at[kv, low], y_up))
        y_far.append(remote(gathered[3].at[kv, high], gathered[2].at[kv, high], y_down))
    pick(1)
    pick(2)
    z_send(1)
    halo_copies = []
    for kv in range(2):
        halo_copies.append(remote(kv_own.at[kv], halo.at[0, kv], after))
        halo_copies.append(remote(kv_own.at[kv], halo.at[1, kv], before))

    part_rows = rows // 2

    def attend(keys_of, values_of, adjust, count, first=False):
        @pl.loop(0, 2 * heads)
        def _(step):
            h = step // 2
            part = step % 2
            lanes = pl.ds(pl.multiple_of(h * HD, HD), HD)
            at = pl.ds(pl.multiple_of(part * part_rows, part_rows), part_rows)
            q = q_buf[h, at]
            scores = lax.dot_general(
                q, keys_of(lanes), (((1,), (1,)), ((), ())), preferred_element_type=jnp.float32
            )
            pieces = [
                adjust(i, scores[:, i * BLOCK : (i + 1) * BLOCK] * SCALE, part) for i in range(count)
            ]
            top = functools.reduce(jnp.maximum, pieces)
            top = jnp.broadcast_to(jnp.max(top, axis=1, keepdims=True), (part_rows, HD))
            if not first:
                old = m_buf[h, at]
                top = jnp.maximum(top, old)
                keep = jnp.exp2(old - top)
            pieces = [jnp.exp2(piece - top) for piece in pieces]
            total_new = functools.reduce(jnp.add, pieces)
            mixed = jnp.dot(
                jnp.concatenate([piece.astype(jnp.bfloat16) for piece in pieces], axis=1),
                values_of(lanes),
                preferred_element_type=jnp.float32,
            )
            m_buf[h, at] = top
            if first:
                l_buf[h, at] = total_new
                acc_buf[h, at] = mixed
            else:
                l_buf[h, at] = l_buf[h, at] * keep + total_new
                acc_buf[h, at] = acc_buf[h, at] * keep + mixed

    row_at = lax.broadcasted_iota(jnp.int32, (part_rows, BLOCK), 0)
    column_at = lax.broadcasted_iota(jnp.int32, (part_rows, BLOCK), 1)

    def radius_of(part):
        low = (tile_level[part * 2] + 1) * rows // 3
        high = (tile_level[part * 2 + 1] + 1) * rows // 3
        return jnp.where(row_at < TILE, low, high)

    def band(offset, exists):
        def adjust(i, piece, part):
            distance = jnp.abs(column_at - row_at + (i * BLOCK + offset - part * part_rows))
            radius = radius_of(part)
            if exists is not None:
                radius = jnp.where(exists, radius, -1)
            return jnp.where(distance <= radius, piece, LOW)

        return adjust

    def slots(places):
        bias = []
        for back, position in places:
            holder = ((z + 4 - back) % 4) * 4 + (y + 4 - COLUMN[position]) % 4
            _, found = wanted(holder, sp)
            bias.append(jnp.where(found > 0, 0.0, LOW).astype(jnp.float32))

        def side(kv):
            return lambda lanes: jnp.concatenate([row[kv, b, p, :, lanes] for b, p in places], axis=0)

        attend(side(0), side(1), lambda i, piece, part: piece + bias[i], len(places))

    def rows_of(ref):
        return lambda lanes: ref[:, lanes]

    attend(rows_of(kv_own.at[0]), rows_of(kv_own.at[1]), band(0, None), 4, first=True)

    for copy in z_copies[0][2] + list(z_far[0]):
        copy.wait_recv()
    slots(((0, 0), (0, 1), (0, 2), (1, 0), (2, 0), (3, 0)))

    z_pass(1)
    for copy in y_far:
        copy.wait_recv()
    pick(3)
    z_send(2)
    for copy in z_copies[1][2]:
        copy.wait_recv()
    slots(((1, 1), (1, 2), (3, 1), (3, 2)))
    z_pass(2)
    for copy in z_far[1]:
        copy.wait_recv()
    slots(((2, 1), (2, 2)))
    for copy in halo_copies:
        copy.wait_recv()
    attend(rows_of(halo.at[0, 0]), rows_of(halo.at[0, 1]), band(-rows, sp > 0), 4)
    attend(rows_of(halo.at[1, 0]), rows_of(halo.at[1, 1]), band(rows, sp < 15), 4)
    for copy in z_copies[2][2] + list(z_far[2]):
        copy.wait_recv()
    slots(((0, 3), (1, 3), (2, 3), (3, 3)))

    @pl.loop(0, heads)
    def _(h):
        lanes = pl.ds(pl.multiple_of(h * HD, HD), HD)
        out[:, lanes] = (acc_buf[h] / jnp.sum(l_buf[h], axis=1, keepdims=True)).astype(out.dtype)

    for copy in copies:
        copy.wait_send()


def body(tokens, w_query, w_key, w_value, cache_keys, cache_values, tile_level, window_map):
    rows, width = tokens.shape
    heads = width // HD
    bf16, f32 = jnp.bfloat16, jnp.float32
    block = (BLOCK, width)
    n_copies = 48
    return pl.pallas_call(
        kernel,
        out_shape=jax.ShapeDtypeStruct((rows, width), bf16),
        in_specs=[pl.BlockSpec(memory_space=pl.ANY)] * 6 + [pl.BlockSpec(memory_space=pltpu.SMEM)] * 2,
        out_specs=pl.BlockSpec(memory_space=pltpu.VMEM),
        scratch_shapes=[
            pltpu.VMEM((4, rows, 2 * width), bf16),
            pltpu.VMEM((4, 2 * width, 3 * width), bf16),
            pltpu.VMEM((rows, 3 * width), f32),
            pltpu.VMEM((heads, rows, HD), bf16),
            pltpu.VMEM((2, rows, width), bf16),
            pltpu.VMEM((2, 2, rows, width), bf16),
            pltpu.VMEM((2, 4) + block, bf16),
            pltpu.VMEM((2, 4) + block, bf16),
            pltpu.VMEM((2, 4) + block, bf16),
            pltpu.VMEM((2, 4) + block, bf16),
            pltpu.VMEM((2, 3, 4) + block, bf16),
            pltpu.VMEM((2, 4, 4) + block, bf16),
            pltpu.VMEM((2, 4) + block, bf16),
            pltpu.VMEM((heads, rows, HD), f32),
            pltpu.VMEM((heads, rows, HD), f32),
            pltpu.VMEM((heads, rows, HD), f32),
            pltpu.SemaphoreType.DMA((4, 3)),
            pltpu.SemaphoreType.DMA((3,)),
            pltpu.SemaphoreType.DMA((n_copies,)),
            pltpu.SemaphoreType.DMA((n_copies,)),
        ],
        compiler_params=pltpu.CompilerParams(
            collective_id=0, has_side_effects=True, vmem_limit_bytes=60 * 1024 * 1024
        ),
    )(tokens, w_query, w_key, w_value, cache_keys, cache_values, tile_level, window_map)


def solution(mesh):
    placed = (
        P("sp", "tp"),
        P(None, "tp"),
        P(None, "tp"),
        P(None, "tp"),
        P("sp", None, "tp"),
        P("sp", None, "tp"),
        P("sp"),
        P(),
    )
    return jax.shard_map(body, mesh=mesh, in_specs=placed, out_specs=P("sp", "tp"), check_vma=False)
```

```python
import functools
import math

import jax
import jax.numpy as jnp
from jax import lax
from jax.experimental import pallas as pl
from jax.experimental.pallas import tpu as pltpu
from jax.sharding import PartitionSpec as P

HD = 128
TILE = 128
BLOCK = 128
MESH = pl.DeviceIdType.MESH
LOW = -1e30
SCALE = math.log2(math.e) / math.sqrt(HD)
COLUMN = (0, 1, 3, 2)
N_COPIES = 64


def kernel(
    tokens, w_query, w_key, w_value, cache_keys, cache_values, tile_level, window_map,
    out,
    tok, weights, total, q_buf, kv_own, halo, k_0, k_1, k_2, k_3, v_0, v_1, v_2, v_3, send, row,
    m_buf, acc_buf, bias_own, bias_halo, turning,
    weight_sem, local_sem, send_sem, recv_sem,
):
    sp = lax.axis_index("sp")
    tp = lax.axis_index("tp")
    z, y = sp // 4, sp % 4
    x, core = tp // 2, tp % 2
    rows, width = tokens.shape
    heads = width // HD
    half = rows // 2
    f32, bf16 = jnp.float32, jnp.bfloat16

    sibling = (sp, x * 2 + 1 - core)
    x_up = (sp, ((x + 1) % 4) * 2 + core)
    x_down = (sp, ((x + 3) % 4) * 2 + core)
    y_up = (z * 4 + (y + 1) % 4, tp)
    y_down = (z * 4 + (y + 3) % 4, tp)
    z_up = (((z + 1) % 4) * 4 + y, tp)
    z_down = (((z + 3) % 4) * 4 + y, tp)
    z_far = (((z + 2) % 4) * 4 + y, tp)
    after = ((sp + 1) % 16, tp)
    before = ((sp + 15) % 16, tp)
    held = ((k_0, v_0), (k_1, v_1), (k_2, v_2), (k_3, v_3))
    peers = (sibling, x_up, x_down, y_up, y_down, z_up, z_down, z_far, after, before)

    barrier = pltpu.get_barrier_semaphore()
    for peer in peers:
        pl.semaphore_signal(barrier, inc=1, device_id=peer, device_id_type=MESH)

    lane = pl.ds(pl.multiple_of(core * width, HD), width)
    own_tokens = pltpu.make_async_copy(tokens, tok.at[0, :, lane], local_sem.at[0])
    own_blocks = [
        pltpu.make_async_copy(cache, held[0][kv], local_sem.at[1 + kv])
        for kv, cache in enumerate((cache_keys, cache_values))
    ]
    own_blocks[0].start()
    own_blocks[1].start()
    own_tokens.start()
    depth = 2 * width
    weight_copies = {}
    for back in (0, 1, 3, 2):
        source = pl.ds(pl.multiple_of(((x + 4 - back) % 4) * depth, depth), depth)
        for j, w in enumerate((w_query, w_key, w_value)):
            copy = pltpu.make_async_copy(
                w.at[source, :], weights.at[back, :, pl.ds(j * width, width)], weight_sem.at[back, j]
            )
            copy.start()
            weight_copies[back, j] = copy

    pl.semaphore_wait(barrier, len(peers))

    copies = []

    def remote(src, dst, peer):
        at = len(copies)
        copy = pltpu.make_async_remote_copy(
            src_ref=src, dst_ref=dst, send_sem=send_sem.at[at], recv_sem=recv_sem.at[at],
            device_id=peer, device_id_type=MESH,
        )
        copy.start()
        copies.append(copy)
        return copy

    y_near = {0: [remote(cache_keys, held[1][0], y_up), remote(cache_keys, held[3][0], y_down)]}
    x_from_down = remote(tokens, tok.at[1, :, lane], x_up)
    x_from_up = remote(tokens, tok.at[3, :, lane], x_down)
    from_sibling = remote(tokens, tok.at[0, :, lane], sibling)
    y_near[1] = [remote(cache_values, held[1][1], y_up), remote(cache_values, held[3][1], y_down)]

    def wanted(holder, owner):
        local, found = jnp.int32(0), jnp.int32(0)
        for k in range(8):
            block = window_map[owner, k]
            hit = jnp.where(block // 4 == holder, 1, 0)
            local = local + hit * (block % 4)
            found = found + hit
        return local, found

    z_copies = {}

    def z_send(kv, first, count):
        for position in range(first, first + count):
            column = COLUMN[position]
            holder = z * 4 + (y + 4 - column) % 4
            for step in range(4):
                local, _ = wanted(holder, ((z + step) % 4) * 4 + y)
                block = held[column][kv][local]
                if step == 0:
                    row[kv, 0, position] = block
                else:
                    send[kv, step - 1, position] = block
        slots = pl.ds(first, count)
        z_copies[kv, first] = [
            remote(send.at[kv, 1, slots], row.at[kv, 2, slots], z_far),
            remote(send.at[kv, 0, slots], row.at[kv, 1, slots], z_up),
            remote(send.at[kv, 2, slots], row.at[kv, 3, slots], z_down),
        ]

    y_far = {}

    def y_pass(kv):
        low, high = pl.ds(0, 2), pl.ds(2, 2)
        for copy in y_near[kv]:
            copy.wait_recv()
        y_far[kv] = [
            remote(held[1][kv].at[low], held[2][kv].at[low], y_up),
            remote(held[3][kv].at[high], held[2][kv].at[high], y_down),
        ]

    def project(back, start):
        for j in range(3):
            weight_copies[back, j].wait()

        @pl.loop(0, 3)
        def _(j):
            columns = pl.ds(pl.multiple_of(j * width, HD), width)
            product = jnp.dot(tok[back], weights[back, :, columns], preferred_element_type=f32)
            if start:
                total[:, columns] = product
            else:
                total[:, columns] += product

    for kv in range(2):
        own_blocks[kv].wait()
        z_send(kv, 0, 1)

    own_tokens.wait()
    from_sibling.wait_recv()
    project(0, True)

    def radius_of(first, count):
        at = lax.broadcasted_iota(jnp.int32, (count, 1), 0) + first
        radius = jnp.zeros((count, 1), jnp.int32)
        for tile in range(rows // TILE):
            radius = jnp.where(at // TILE == tile, (tile_level[tile] + 1) * rows // 3, radius)
        return radius, at

    def bias_of(first, count, key_first, key_count, exists):
        radius, at = radius_of(first, count)
        key_at = lax.broadcasted_iota(jnp.int32, (count, key_count), 1) + key_first
        allowed = jnp.abs(key_at - at) <= radius
        if exists is not None:
            allowed = allowed & exists
        return jnp.where(allowed, 0.0, LOW).astype(f32)

    for part in range(2):
        first = part * half
        bias_own[pl.ds(first, half), :] = bias_of(first, half, 0, rows, None)
        left = rows - first
        bias_halo[part, :, pl.ds(0, left)] = bias_of(first, half, first - rows, left, sp > 0)
        bias_halo[part, :, pl.ds(left, half + first)] = bias_of(first, half, rows, half + first, sp < 15)

    y_pass(0)
    z_send(0, 1, 2)

    x_from_down.wait_recv()
    x_far = [remote(tok.at[1, pl.ds(0, half), lane], tok.at[2, pl.ds(0, half), lane], x_up)]
    x_from_up.wait_recv()
    x_far.append(remote(tok.at[3, pl.ds(half, half), lane], tok.at[2, pl.ds(half, half), lane], x_down))
    sibling_down = remote(tok.at[1, :, lane], tok.at[1, :, lane], sibling)
    sibling_up = remote(tok.at[3, :, lane], tok.at[3, :, lane], sibling)
    sibling_down.wait_recv()
    project(1, False)
    sibling_up.wait_recv()
    project(3, False)
    sibling_far = []
    for part in range(2):
        piece = pl.ds(part * half, half)
        x_far[part].wait_recv()
        sibling_far.append(remote(tok.at[2, piece, lane], tok.at[2, piece, lane], sibling))
    for copy in sibling_far:
        copy.wait_recv()
    project(2, False)

    for h in range(heads):
        for j in range(3):
            part = total[:, pl.ds(j * width + h * HD, HD)].astype(bf16)
            if j == 0:
                q_buf[h] = part
            else:
                kv_own[j - 1, h] = part

    y_pass(1)
    z_send(1, 1, 2)
    halo_copies = {}
    turns = []

    def describe(src, dst, send_at, recv_at, peer):
        return pltpu.make_async_remote_copy(
            src_ref=src, dst_ref=dst, send_sem=send_sem.at[send_at], recv_sem=recv_sem.at[recv_at],
            device_id=peer, device_id_type=MESH,
        )

    for h in range(heads):
        halo_copies[h] = []
        for side, peer in ((0, after), (1, before)):
            halo_copies[h].append(remote(kv_own.at[0, h], halo.at[side, 0, h], peer))
        turn_at = N_COPIES - 1 - h
        for side, peer, last, z_next, y_next in ((0, after, 3, z_up, y_up), (1, before, 0, z_down, y_down)):
            at = len(copies)
            source, place = kv_own.at[1, h], halo.at[side, 1, h]
            straight = describe(source, place, at, at, peer)
            turn = describe(source, turning.at[h], at, turn_at, z_next)
            onward = describe(turning.at[h], place, turn_at, at, y_next)
            copies.append(straight)
            halo_copies[h].append(straight)
            turns.append((last, turn, onward))

            @pl.when(y != last)
            def _():
                straight.start()

            @pl.when(y == last)
            def _():
                turn.start()

    def turn_values():
        for last, turn, onward in turns:

            @pl.when(y == last)
            def _():
                turn.wait_recv()
                onward.start()

    ones = jnp.ones((BLOCK, HD), bf16)

    def attend(h, at, scores, values, count, first=False):
        pieces = [scores[:, i * BLOCK : (i + 1) * BLOCK] for i in range(count)]
        top = functools.reduce(jnp.maximum, pieces)
        top = jnp.broadcast_to(jnp.max(top, axis=1, keepdims=True), pieces[0].shape)
        if not first:
            old = m_buf[h, at]
            top = jnp.maximum(top, old)
            keep = jnp.exp2((old - top) * SCALE)
        scaled = top * SCALE
        weight = jnp.concatenate(
            [jnp.exp2(piece * SCALE - scaled).astype(bf16) for piece in pieces], axis=1
        )
        values = jnp.concatenate([values, jnp.concatenate([ones] * count, axis=0)], axis=1)
        mixed = jnp.dot(weight, values, preferred_element_type=f32)
        m_buf[h, at] = top
        for side in range(2):
            lanes = pl.ds(side * HD, HD)
            part = mixed[:, side * HD : (side + 1) * HD]
            acc_buf[h, at, lanes] = part if first else acc_buf[h, at, lanes] * keep + part

    contract = (((1,), (1,)), ((), ()))

    def slots(places):
        everything = pl.ds(0, rows)
        count = len(places)
        first_lane = lax.broadcasted_iota(jnp.int32, (BLOCK, HD), 1) == 0
        bias = []
        for back, position in places:
            holder = ((z + 4 - back) % 4) * 4 + (y + 4 - COLUMN[position]) % 4
            _, found = wanted(holder, sp)
            low = jnp.where(found > 0, 0.0, LOW).astype(f32)
            bias.append(jnp.where(first_lane, low, 0.0).astype(bf16))
        bias = jnp.concatenate(bias, axis=0)
        pointer = jnp.where(lax.broadcasted_iota(jnp.int32, (rows, HD), 1) == 0, 1.0, 0.0).astype(bf16)
        for h in range(heads):
            lanes = pl.ds(h * HD, HD)
            keys = jnp.concatenate([row[0, b, p, :, lanes] for b, p in places], axis=0)
            values = jnp.concatenate([row[1, b, p, :, lanes] for b, p in places], axis=0)
            scores = lax.dot_general(
                jnp.concatenate([q_buf[h], pointer], axis=1),
                jnp.concatenate([keys, bias], axis=1),
                contract,
                preferred_element_type=f32,
            )
            attend(h, everything, scores, values, count)

    for h in range(heads):
        scores = lax.dot_general(q_buf[h], kv_own[0, h], contract, preferred_element_type=f32)
        attend(h, pl.ds(0, rows), scores + bias_own[...], kv_own[1, h], 4, first=True)

    for copy in y_far[0]:
        copy.wait_recv()
    z_send(0, 3, 1)
    for copy in z_copies[0, 0] + z_copies[1, 0]:
        copy.wait_recv()
    slots(((0, 0), (0, 1), (0, 2), (1, 0), (2, 0), (3, 0)))
    for copy in y_far[1]:
        copy.wait_recv()
    z_send(1, 3, 1)
    for copy in z_copies[0, 1] + z_copies[1, 1]:
        copy.wait_recv()
    slots(((1, 1), (1, 2), (2, 1), (2, 2), (3, 1), (3, 2)))
    turn_values()
    for copy in z_copies[0, 3] + z_copies[1, 3]:
        copy.wait_recv()
    slots(((0, 3), (1, 3), (2, 3), (3, 3)))

    for h in range(heads):
        for copy in halo_copies[h]:
            copy.wait_recv()
        for part in range(2):
            at = pl.ds(part * half, half)
            left = pl.ds(part * half, rows - part * half)
            right = pl.ds(0, half + part * half)
            keys = jnp.concatenate([halo[0, 0, h, left], halo[1, 0, h, right]], axis=0)
            values = jnp.concatenate([halo[0, 1, h, left], halo[1, 1, h, right]], axis=0)
            scores = lax.dot_general(q_buf[h, at], keys, contract, preferred_element_type=f32)
            attend(h, at, scores + bias_halo[part], values, 6)
        sums = acc_buf[h]
        out[:, pl.ds(h * HD, HD)] = (sums[:, :HD] / sums[:, HD:]).astype(out.dtype)

    for copy in copies:
        copy.wait_send()
    for last, _, onward in turns:

        @pl.when(y == last)
        def _():
            onward.wait_send()


def body(tokens, w_query, w_key, w_value, cache_keys, cache_values, tile_level, window_map):
    rows, width = tokens.shape
    heads = width // HD
    bf16, f32 = jnp.bfloat16, jnp.float32
    block = (BLOCK, width)
    return pl.pallas_call(
        kernel,
        out_shape=jax.ShapeDtypeStruct((rows, width), bf16),
        in_specs=[pl.BlockSpec(memory_space=pl.ANY)] * 6 + [pl.BlockSpec(memory_space=pltpu.SMEM)] * 2,
        out_specs=pl.BlockSpec(memory_space=pltpu.VMEM),
        scratch_shapes=[
            pltpu.VMEM((4, rows, 2 * width), bf16),
            pltpu.VMEM((4, 2 * width, 3 * width), bf16),
            pltpu.VMEM((rows, 3 * width), f32),
            pltpu.VMEM((heads, rows, HD), bf16),
            pltpu.VMEM((2, heads, rows, HD), bf16),
            pltpu.VMEM((2, 2, heads, rows, HD), bf16),
            pltpu.VMEM((4,) + block, bf16),
            pltpu.VMEM((4,) + block, bf16),
            pltpu.VMEM((4,) + block, bf16),
            pltpu.VMEM((4,) + block, bf16),
            pltpu.VMEM((4,) + block, bf16),
            pltpu.VMEM((4,) + block, bf16),
            pltpu.VMEM((4,) + block, bf16),
            pltpu.VMEM((4,) + block, bf16),
            pltpu.VMEM((2, 3, 4) + block, bf16),
            pltpu.VMEM((2, 4, 4) + block, bf16),
            pltpu.VMEM((heads, rows, HD), f32),
            pltpu.VMEM((heads, rows, 2 * HD), f32),
            pltpu.VMEM((rows, rows), f32),
            pltpu.VMEM((2, rows // 2, 3 * rows // 2), f32),
            pltpu.VMEM((heads, rows, HD), bf16),
            pltpu.SemaphoreType.DMA((4, 3)),
            pltpu.SemaphoreType.DMA((3,)),
            pltpu.SemaphoreType.DMA((N_COPIES,)),
            pltpu.SemaphoreType.DMA((N_COPIES,)),
        ],
        compiler_params=pltpu.CompilerParams(
            collective_id=0, has_side_effects=True, vmem_limit_bytes=62 * 1024 * 1024
        ),
    )(tokens, w_query, w_key, w_value, cache_keys, cache_values, tile_level, window_map)


def solution(mesh):
    placed = (
        P("sp", "tp"),
        P(None, "tp"),
        P(None, "tp"),
        P(None, "tp"),
        P("sp", None, "tp"),
        P("sp", None, "tp"),
        P("sp"),
        P(),
    )
    return jax.shard_map(body, mesh=mesh, in_specs=placed, out_specs=P("sp", "tp"), check_vma=False)
```

```python
import functools
import math

import jax
import jax.numpy as jnp
from jax import lax
from jax.experimental import pallas as pl
from jax.experimental.pallas import tpu as pltpu
from jax.sharding import PartitionSpec as P

HD = 128
TILE = 128
BLOCK = 128
MESH = pl.DeviceIdType.MESH
LOW = -1e30
SCALE = math.log2(math.e) / math.sqrt(HD)
COLUMN = (0, 1, 3, 2)
N_COPIES = 96


def kernel(
    tokens, w_query, w_key, w_value, cache_keys, cache_values, tile_level, window_map,
    out,
    tok, tok_near, weights, total, q_buf, kv_own, kv_far, k_0, k_1, k_2, k_3, v_0, v_1, v_2, v_3, send, row,
    m_buf, acc_buf, bias_own, bias_near, bias_far, turning,
    weight_sem, local_sem, out_sem, send_sem, recv_sem,
):
    sp = lax.axis_index("sp")
    tp = lax.axis_index("tp")
    z, y = sp // 4, sp % 4
    x, core = tp // 2, tp % 2
    rows, width = tokens.shape
    heads = width // HD
    half = rows // 2
    f32, bf16 = jnp.float32, jnp.bfloat16

    sibling = (sp, x * 2 + 1 - core)
    x_up = (sp, ((x + 1) % 4) * 2 + core)
    x_down = (sp, ((x + 3) % 4) * 2 + core)
    y_up = (z * 4 + (y + 1) % 4, tp)
    y_down = (z * 4 + (y + 3) % 4, tp)
    z_up = (((z + 1) % 4) * 4 + y, tp)
    z_down = (((z + 3) % 4) * 4 + y, tp)
    z_far = (((z + 2) % 4) * 4 + y, tp)
    after = ((sp + 1) % 16, tp)
    before = ((sp + 15) % 16, tp)
    held = ((k_0, v_0), (k_1, v_1), (k_2, v_2), (k_3, v_3))
    peers = (sibling, x_up, x_down, y_up, y_down, z_up, z_down, z_far, after, before)

    barrier = pltpu.get_barrier_semaphore()
    for peer in peers:
        pl.semaphore_signal(barrier, inc=1, device_id=peer, device_id_type=MESH)

    lane = pl.ds(pl.multiple_of(core * width, HD), width)
    own_tokens = pltpu.make_async_copy(tokens, tok.at[0, :, lane], local_sem.at[0])
    own_blocks = [
        pltpu.make_async_copy(cache, held[0][kv], local_sem.at[1 + kv])
        for kv, cache in enumerate((cache_keys, cache_values))
    ]
    own_blocks[0].start()
    own_blocks[1].start()
    own_tokens.start()
    pl.semaphore_wait(barrier, len(peers))

    copies = []

    def remote(src, dst, peer):
        at = len(copies)
        copy = pltpu.make_async_remote_copy(
            src_ref=src, dst_ref=dst, send_sem=send_sem.at[at], recv_sem=recv_sem.at[at],
            device_id=peer, device_id_type=MESH,
        )
        copy.start()
        copies.append(copy)
        return copy

    halves = (pl.ds(0, half), pl.ds(half, half))

    class Spread:
        def __init__(self, buf, source):
            self.buf = buf
            self.near = [
                remote(source, buf.at[1, :, lane], x_up),
                remote(source, buf.at[3, :, lane], x_down),
                remote(source, buf.at[0, :, lane], sibling),
            ]

        def pass_near(self):
            buf = self.buf
            self.far = []
            for part, back, peer in ((0, 1, x_up), (1, 3, x_down)):
                self.near[part].wait_recv()
                piece = halves[part]
                self.far.append(remote(buf.at[back, piece, lane], buf.at[2, piece, lane], peer))
            self.near_sibling = {
                back: remote(buf.at[back, :, lane], buf.at[back, :, lane], sibling) for back in (1, 3)
            }

        def pass_far(self):
            buf = self.buf
            self.far_sibling = []
            for part in range(2):
                self.far[part].wait_recv()
                piece = halves[part]
                self.far_sibling.append(remote(buf.at[2, piece, lane], buf.at[2, piece, lane], sibling))

    y_near = {0: [remote(cache_keys, held[1][0], y_up), remote(cache_keys, held[3][0], y_down)]}
    own_spread = Spread(tok, tokens)
    y_near[1] = [remote(cache_values, held[1][1], y_up), remote(cache_values, held[3][1], y_down)]
    near_tokens = [
        remote(tokens.at[halves[1], :], tok_near.at[0, halves[0], lane], after),
        remote(tokens.at[halves[0], :], tok_near.at[0, halves[1], lane], before),
    ]

    depth = 2 * width
    weight_copies = {}
    for back in (0, 1, 3, 2):
        source = pl.ds(pl.multiple_of(((x + 4 - back) % 4) * depth, depth), depth)
        for j, w in enumerate((w_query, w_key, w_value)):
            copy = pltpu.make_async_copy(
                w.at[source, :], weights.at[back, :, pl.ds(j * width, width)], weight_sem.at[back, j]
            )
            copy.start()
            weight_copies[back, j] = copy

    def wanted(holder, owner):
        local, found = jnp.int32(0), jnp.int32(0)
        for k in range(8):
            block = window_map[k, owner]
            hit = jnp.where(block // 4 == holder, 1, 0)
            local = local + hit * (block % 4)
            found = found + hit
        return local, found

    z_copies = {}

    def z_send(kv, first, count):
        for position in range(first, first + count):
            column = COLUMN[position]
            holder = z * 4 + (y + 4 - column) % 4
            for step in range(4):
                local, _ = wanted(holder, ((z + step) % 4) * 4 + y)
                block = held[column][kv][local]
                if step == 0:
                    row[kv, 0, position] = block
                else:
                    send[kv, step - 1, position] = block
        slots = pl.ds(first, count)
        z_copies[kv, first] = [
            remote(send.at[kv, 1, slots], row.at[kv, 2, slots], z_far),
            remote(send.at[kv, 0, slots], row.at[kv, 1, slots], z_up),
            remote(send.at[kv, 2, slots], row.at[kv, 3, slots], z_down),
        ]

    y_far = {}

    def y_pass(kv):
        low, high = pl.ds(0, 2), pl.ds(2, 2)
        for copy in y_near[kv]:
            copy.wait_recv()
        y_far[kv] = [
            remote(held[1][kv].at[low], held[2][kv].at[low], y_up),
            remote(held[3][kv].at[high], held[2][kv].at[high], y_down),
        ]

    def project(buf, back, first, start):
        @pl.loop(first, 3)
        def _(j):
            source = pl.ds(pl.multiple_of(j * width, HD), width)
            columns = pl.ds(pl.multiple_of((j - first) * width, HD), width)
            product = jnp.dot(buf[back], weights[back, :, source], preferred_element_type=f32)
            if start:
                total[:, columns] = product
            else:
                total[:, columns] += product

    def project_own(back, start=False):
        for j in range(3):
            weight_copies[back, j].wait()
        project(tok, back, 0, start)

    for kv in range(2):
        own_blocks[kv].wait()
        z_send(kv, 0, 1)

    own_tokens.wait()
    own_spread.near[2].wait_recv()
    project_own(0, True)

    def radius_of(first, count):
        at = lax.broadcasted_iota(jnp.int32, (count, 1), 0) + first
        radius = jnp.zeros((count, 1), jnp.int32)
        for tile in range(rows // TILE):
            radius = jnp.where(at // TILE == tile, (tile_level[tile] + 1) * rows // 3, radius)
        return radius, at

    def bias_of(first, count, key_first, key_count, exists):
        radius, at = radius_of(first, count)
        key_at = lax.broadcasted_iota(jnp.int32, (count, key_count), 1) + key_first
        allowed = jnp.abs(key_at - at) <= radius
        if exists is not None:
            allowed = allowed & exists
        return jnp.where(allowed, 0.0, LOW).astype(f32)

    for part in range(2):
        first = part * half
        bias_own[halves[part], :] = bias_of(first, half, 0, rows, None)
        bias_near[halves[part], halves[0]] = bias_of(first, half, -half, half, sp > 0)
        bias_near[halves[part], halves[1]] = bias_of(first, half, rows, half, sp < 15)
    bias_far[0] = bias_of(0, half, -rows, half, sp > 0)
    bias_far[1] = bias_of(half, half, rows + half, half, sp < 15)

    own_spread.pass_near()
    y_pass(0)
    z_send(0, 1, 2)

    for back in (1, 3):
        own_spread.near_sibling[back].wait_recv()
        project_own(back)
    own_spread.pass_far()
    y_pass(1)
    z_send(1, 1, 2)
    for copy in own_spread.far_sibling:
        copy.wait_recv()
    project_own(2)

    for h in range(heads):
        for j in range(3):
            part = total[:, pl.ds(j * width + h * HD, HD)].astype(bf16)
            if j == 0:
                q_buf[h] = part
            else:
                kv_own[j - 1, h] = part

    far_copies = {}
    turns = []

    def describe(src, dst, send_at, recv_at, peer):
        return pltpu.make_async_remote_copy(
            src_ref=src, dst_ref=dst, send_sem=send_sem.at[send_at], recv_sem=recv_sem.at[recv_at],
            device_id=peer, device_id_type=MESH,
        )

    sides = ((0, after, 3, z_up, y_up), (1, before, 0, z_down, y_down))
    for h in range(heads):
        far_copies[h] = []
        for kv in range(2):
            turned = kv == 1 or h < 2
            if turned:
                slot = len(turns) // 2
            for side, peer, last, z_next, y_next in sides:
                source, place = kv_own.at[kv, h, halves[side]], kv_far.at[side, kv, h]
                if not turned:
                    far_copies[h].append(remote(source, place, peer))
                    continue
                at, turn_at = len(copies), N_COPIES - 1 - slot
                straight = describe(source, place, at, at, peer)
                turn = describe(source, turning.at[slot], at, turn_at, z_next)
                onward = describe(turning.at[slot], place, turn_at, at, y_next)
                copies.append(straight)
                far_copies[h].append(straight)
                turns.append((last, turn, onward))

                @pl.when(y != last)
                def _():
                    straight.start()

                @pl.when(y == last)
                def _():
                    turn.start()

    def pass_turned():
        for last, turn, onward in turns:

            @pl.when(y == last)
            def _():
                turn.wait_recv()
                onward.start()

    ones = jnp.ones((BLOCK, HD), bf16)

    def attend(h, at, scores, values, count, first=False):
        pieces = [scores[:, i * BLOCK : (i + 1) * BLOCK] for i in range(count)]
        top = functools.reduce(jnp.maximum, pieces)
        top = jnp.broadcast_to(jnp.max(top, axis=1, keepdims=True), pieces[0].shape)
        if not first:
            old = m_buf[h, at]
            top = jnp.maximum(top, old)
            keep = jnp.exp2((old - top) * SCALE)
        scaled = top * SCALE
        weight = jnp.concatenate(
            [jnp.exp2(piece * SCALE - scaled).astype(bf16) for piece in pieces], axis=1
        )
        values = jnp.concatenate([values, jnp.concatenate([ones] * count, axis=0)], axis=1)
        mixed = jnp.dot(weight, values, preferred_element_type=f32)
        m_buf[h, at] = top
        for side in range(2):
            lanes = pl.ds(side * HD, HD)
            part = mixed[:, side * HD : (side + 1) * HD]
            acc_buf[h, at, lanes] = part if first else acc_buf[h, at, lanes] * keep + part

    contract = (((1,), (1,)), ((), ()))

    def slots(places):
        everything = pl.ds(0, rows)
        count = len(places)
        first_lane = lax.broadcasted_iota(jnp.int32, (BLOCK, HD), 1) == 0
        bias = []
        for back, position in places:
            holder = ((z + 4 - back) % 4) * 4 + (y + 4 - COLUMN[position]) % 4
            _, found = wanted(holder, sp)
            low = jnp.where(found > 0, 0.0, LOW).astype(f32)
            bias.append(jnp.where(first_lane, low, 0.0).astype(bf16))
        bias = jnp.concatenate(bias, axis=0)
        pointer = jnp.where(lax.broadcasted_iota(jnp.int32, (rows, HD), 1) == 0, 1.0, 0.0).astype(bf16)
        for h in range(heads):
            lanes = pl.ds(h * HD, HD)
            keys = jnp.concatenate([row[0, b, p, :, lanes] for b, p in places], axis=0)
            values = jnp.concatenate([row[1, b, p, :, lanes] for b, p in places], axis=0)
            scores = lax.dot_general(
                jnp.concatenate([q_buf[h], pointer], axis=1),
                jnp.concatenate([keys, bias], axis=1),
                contract,
                preferred_element_type=f32,
            )
            attend(h, everything, scores, values, count)

    def rows_of(part, bias, first=False):
        for h in range(heads):
            scores = lax.dot_general(q_buf[h], part(0, h), contract, preferred_element_type=f32)
            attend(h, pl.ds(0, rows), scores + bias[...], part(1, h), 4, first)

    rows_of(lambda kv, h: kv_own[kv, h], bias_own, first=True)

    for copy in near_tokens:
        copy.wait_recv()
    near_spread = Spread(tok_near, tok_near.at[0, :, lane])
    for copy in z_copies[0, 0] + z_copies[1, 0]:
        copy.wait_recv()
    slots(((0, 0), (0, 1), (0, 2), (1, 0), (2, 0), (3, 0)))
    near_spread.near[2].wait_recv()
    project(tok_near, 0, 1, True)

    for copy in y_far[0]:
        copy.wait_recv()
    z_send(0, 3, 1)
    for copy in y_far[1]:
        copy.wait_recv()
    z_send(1, 3, 1)

    near_spread.pass_near()
    for back in (1, 3):
        near_spread.near_sibling[back].wait_recv()
        project(tok_near, back, 1, False)
    pass_turned()
    near_spread.pass_far()
    for copy in z_copies[0, 1] + z_copies[1, 1]:
        copy.wait_recv()
    slots(((1, 1), (1, 2), (2, 1), (2, 2), (3, 1), (3, 2)))
    for copy in near_spread.far_sibling:
        copy.wait_recv()
    project(tok_near, 2, 1, False)
    tok[0] = total[:, : 2 * width].astype(bf16)
    rows_of(lambda kv, h: tok[0, :, pl.ds(kv * width + h * HD, HD)], bias_near)

    for h in range(heads):
        for copy in far_copies[h]:
            copy.wait_recv()
        for side in range(2):
            at = halves[side]
            scores = lax.dot_general(q_buf[h, at], kv_far[side, 0, h], contract, preferred_element_type=f32)
            attend(h, at, scores + bias_far[side], kv_far[side, 1, h], 2)

    for copy in z_copies[0, 3] + z_copies[1, 3]:
        copy.wait_recv()
    slots(((0, 3), (1, 3), (2, 3), (3, 3)))

    out_copies = []
    for h in range(heads):
        sums = acc_buf[h]
        lanes = pl.ds(h * HD, HD)
        q_buf[h] = (sums[:, :HD] / sums[:, HD:]).astype(out.dtype)
        out_copies.append(pltpu.make_async_copy(q_buf.at[h], out.at[:, lanes], out_sem.at[h]))
        out_copies[h].start()
    for copy in out_copies:
        copy.wait()

    for copy in copies:
        copy.wait_send()
    for last, _, onward in turns:

        @pl.when(y == last)
        def _():
            onward.wait_send()


def body(tokens, w_query, w_key, w_value, cache_keys, cache_values, tile_level, window_map):
    rows, width = tokens.shape
    heads = width // HD
    bf16, f32 = jnp.bfloat16, jnp.float32
    block = (BLOCK, width)
    return pl.pallas_call(
        kernel,
        out_shape=jax.ShapeDtypeStruct((rows, width), bf16),
        in_specs=[pl.BlockSpec(memory_space=pl.ANY)] * 6 + [pl.BlockSpec(memory_space=pltpu.SMEM)] * 2,
        out_specs=pl.BlockSpec(memory_space=pl.ANY),
        scratch_shapes=[
            pltpu.VMEM((4, rows, 2 * width), bf16),
            pltpu.VMEM((4, rows, 2 * width), bf16),
            pltpu.VMEM((4, 2 * width, 3 * width), bf16),
            pltpu.VMEM((rows, 3 * width), f32),
            pltpu.VMEM((heads, rows, HD), bf16),
            pltpu.VMEM((2, heads, rows, HD), bf16),
            pltpu.VMEM((2, 2, heads, rows // 2, HD), bf16),
            pltpu.VMEM((4,) + block, bf16),
            pltpu.VMEM((4,) + block, bf16),
            pltpu.VMEM((4,) + block, bf16),
            pltpu.VMEM((4,) + block, bf16),
            pltpu.VMEM((4,) + block, bf16),
            pltpu.VMEM((4,) + block, bf16),
            pltpu.VMEM((4,) + block, bf16),
            pltpu.VMEM((4,) + block, bf16),
            pltpu.VMEM((2, 3, 4) + block, bf16),
            pltpu.VMEM((2, 4, 4) + block, bf16),
            pltpu.VMEM((heads, rows, HD), f32),
            pltpu.VMEM((heads, rows, 2 * HD), f32),
            pltpu.VMEM((rows, rows), f32),
            pltpu.VMEM((rows, rows), f32),
            pltpu.VMEM((2, rows // 2, rows // 2), f32),
            pltpu.VMEM((7, rows // 2, HD), bf16),
            pltpu.SemaphoreType.DMA((4, 3)),
            pltpu.SemaphoreType.DMA((3,)),
            pltpu.SemaphoreType.DMA((heads,)),
            pltpu.SemaphoreType.DMA((N_COPIES,)),
            pltpu.SemaphoreType.DMA((N_COPIES,)),
        ],
        compiler_params=pltpu.CompilerParams(
            collective_id=0, has_side_effects=True, vmem_limit_bytes=63 * 1024 * 1024
        ),
    )(tokens, w_query, w_key, w_value, cache_keys, cache_values, tile_level, window_map.T)


def solution(mesh):
    placed = (
        P("sp", "tp"),
        P(None, "tp"),
        P(None, "tp"),
        P(None, "tp"),
        P("sp", None, "tp"),
        P("sp", None, "tp"),
        P("sp"),
        P(),
    )
    return jax.shard_map(body, mesh=mesh, in_specs=placed, out_specs=P("sp", "tp"), check_vma=False)
```

```python
import functools
import math

import jax
import jax.numpy as jnp
from jax import lax
from jax.experimental import pallas as pl
from jax.experimental.pallas import tpu as pltpu
from jax.sharding import PartitionSpec as P

HD = 128
TILE = 128
BLOCK = 128
MESH = pl.DeviceIdType.MESH
LOW = -1e30
SCALE = math.log2(math.e) / math.sqrt(HD)
COLUMN = (0, 1, 3, 2)
N_COPIES = 60


def kernel(
    tokens, w_query, w_key, w_value, cache_keys, cache_values, tile_level, window_map,
    out,
    tok, tok_near, weights, total, q_buf, kv_own, kv_far, k_0, k_1, k_2, k_3, v_0, v_1, v_2, v_3, send, row,
    m_buf, acc_buf, bias_own, bias_near, bias_far, turning,
    weight_sem, local_sem, out_sem, send_sem, recv_sem,
):
    sp = lax.axis_index("sp")
    tp = lax.axis_index("tp")
    z, y = sp // 4, sp % 4
    x, core = tp // 2, tp % 2
    rows, width = tokens.shape
    heads = width // HD
    half = rows // 2
    f32, bf16 = jnp.float32, jnp.bfloat16

    sibling = (sp, x * 2 + 1 - core)
    x_up = (sp, ((x + 1) % 4) * 2 + core)
    x_down = (sp, ((x + 3) % 4) * 2 + core)
    y_up = (z * 4 + (y + 1) % 4, tp)
    y_down = (z * 4 + (y + 3) % 4, tp)
    z_up = (((z + 1) % 4) * 4 + y, tp)
    z_down = (((z + 3) % 4) * 4 + y, tp)
    z_far = (((z + 2) % 4) * 4 + y, tp)
    after = ((sp + 1) % 16, tp)
    before = ((sp + 15) % 16, tp)
    held = ((k_0, v_0), (k_1, v_1), (k_2, v_2), (k_3, v_3))
    peers = (sibling, x_up, x_down, y_up, y_down, z_up, z_down, z_far, after, before)

    barrier = pltpu.get_barrier_semaphore()
    for peer in peers:
        pl.semaphore_signal(barrier, inc=1, device_id=peer, device_id_type=MESH)

    lane = pl.ds(pl.multiple_of(core * width, HD), width)
    own_tokens = pltpu.make_async_copy(tokens, tok.at[0, :, lane], local_sem.at[0])
    own_blocks = [
        pltpu.make_async_copy(cache, held[0][kv], local_sem.at[1 + kv])
        for kv, cache in enumerate((cache_keys, cache_values))
    ]
    own_blocks[0].start()
    own_blocks[1].start()
    own_tokens.start()
    pl.semaphore_wait(barrier, len(peers))

    copies = []

    def remote(src, dst, peer):
        at = len(copies)
        copy = pltpu.make_async_remote_copy(
            src_ref=src, dst_ref=dst, send_sem=send_sem.at[at], recv_sem=recv_sem.at[at],
            device_id=peer, device_id_type=MESH,
        )
        copy.start()
        copies.append(copy)
        return copy

    halves = (pl.ds(0, half), pl.ds(half, half))

    class Spread:
        def __init__(self, buf, source):
            self.buf = buf
            self.near = [
                remote(source, buf.at[1, :, lane], x_up),
                remote(source, buf.at[3, :, lane], x_down),
                remote(source, buf.at[0, :, lane], sibling),
            ]

        def pass_near(self):
            buf = self.buf
            self.far = []
            for part, back, peer in ((0, 1, x_up), (1, 3, x_down)):
                self.near[part].wait_recv()
                piece = halves[part]
                self.far.append(remote(buf.at[back, piece, lane], buf.at[2, piece, lane], peer))
            self.near_sibling = {
                back: remote(buf.at[back, :, lane], buf.at[back, :, lane], sibling) for back in (1, 3)
            }

        def pass_far(self):
            buf = self.buf
            self.far_sibling = []
            for part in range(2):
                self.far[part].wait_recv()
                piece = halves[part]
                self.far_sibling.append(remote(buf.at[2, piece, lane], buf.at[2, piece, lane], sibling))

    y_near = {0: [remote(cache_keys, held[1][0], y_up), remote(cache_keys, held[3][0], y_down)]}
    own_spread = Spread(tok, tokens)
    near_tokens = [
        remote(tokens.at[halves[1], :], tok_near.at[0, halves[0], lane], after),
        remote(tokens.at[halves[0], :], tok_near.at[0, halves[1], lane], before),
    ]
    y_near[1] = [remote(cache_values, held[1][1], y_up), remote(cache_values, held[3][1], y_down)]

    depth = 2 * width
    weight_copies = {}
    for back in (0, 1, 3, 2):
        source = pl.ds(pl.multiple_of(((x + 4 - back) % 4) * depth, depth), depth)
        for j, w in enumerate((w_query, w_key, w_value)):
            copy = pltpu.make_async_copy(
                w.at[source, :], weights.at[back, :, pl.ds(j * width, width)], weight_sem.at[back, j]
            )
            copy.start()
            weight_copies[back, j] = copy

    def wanted(holder, owner):
        local, found = jnp.int32(0), jnp.int32(0)
        for k in range(8):
            block = window_map[k, owner]
            hit = jnp.where(block // 4 == holder, 1, 0)
            local = local + hit * (block % 4)
            found = found + hit
        return local, found

    z_copies = {}

    def z_send(kv, first, count):
        for position in range(first, first + count):
            column = COLUMN[position]
            holder = z * 4 + (y + 4 - column) % 4
            for step in range(4):
                local, _ = wanted(holder, ((z + step) % 4) * 4 + y)
                block = held[column][kv][local]
                if step == 0:
                    row[kv, 0, position] = block
                else:
                    send[kv, step - 1, position] = block
        slots = pl.ds(first, count)
        z_copies[kv, first] = [
            remote(send.at[kv, 1, slots], row.at[kv, 2, slots], z_far),
            remote(send.at[kv, 0, slots], row.at[kv, 1, slots], z_up),
            remote(send.at[kv, 2, slots], row.at[kv, 3, slots], z_down),
        ]

    y_far = {}

    def y_pass(kv):
        low, high = pl.ds(0, 2), pl.ds(2, 2)
        for copy in y_near[kv]:
            copy.wait_recv()
        y_far[kv] = [
            remote(held[1][kv].at[low], held[2][kv].at[low], y_up),
            remote(held[3][kv].at[high], held[2][kv].at[high], y_down),
        ]

    def project(buf, back, first, start):
        wide = (3 - first) * width
        for at in range(0, wide, 2 * HD):
            columns = pl.ds(at, min(2 * HD, wide - at))
            source = pl.ds(first * width + at, min(2 * HD, wide - at))
            product = jnp.dot(buf[back], weights[back, :, source], preferred_element_type=f32)
            if start:
                total[:, columns] = product
            else:
                total[:, columns] += product

    def project_own(back, start=False):
        for j in range(3):
            weight_copies[back, j].wait()
        project(tok, back, 0, start)

    for kv in range(2):
        own_blocks[kv].wait()
        z_send(kv, 0, 1)

    own_tokens.wait()
    own_spread.near[2].wait_recv()
    project_own(0, True)

    def radius_of(first, count):
        at = lax.broadcasted_iota(jnp.int32, (count, 1), 0) + first
        radius = jnp.zeros((count, 1), jnp.int32)
        for tile in range(rows // TILE):
            radius = jnp.where(at // TILE == tile, (tile_level[tile] + 1) * rows // 3, radius)
        return radius, at

    def bias_of(first, count, key_first, key_count, exists):
        radius, at = radius_of(first, count)
        key_at = lax.broadcasted_iota(jnp.int32, (count, key_count), 1) + key_first
        allowed = jnp.abs(key_at - at) <= radius
        if exists is not None:
            allowed = allowed & exists
        return jnp.where(allowed, 0.0, LOW).astype(f32)

    for part in range(2):
        first = part * half
        bias_own[halves[part], :] = bias_of(first, half, 0, rows, None)
        bias_near[halves[part], halves[0]] = bias_of(first, half, -half, half, sp > 0)
        bias_near[halves[part], halves[1]] = bias_of(first, half, rows, half, sp < 15)
    bias_far[0] = bias_of(0, half, -rows, half, sp > 0)
    bias_far[1] = bias_of(half, half, rows + half, half, sp < 15)

    own_spread.pass_near()
    y_pass(0)
    z_send(0, 1, 2)

    for back in (1, 3):
        own_spread.near_sibling[back].wait_recv()
        project_own(back)
    own_spread.pass_far()
    for copy in near_tokens:
        copy.wait_recv()
    near_spread = Spread(tok_near, tok_near.at[0, :, lane])
    for copy in own_spread.far_sibling:
        copy.wait_recv()
    project_own(2)

    for h in range(heads):
        for j in range(3):
            part = total[:, pl.ds(j * width + h * HD, HD)].astype(bf16)
            if j == 0:
                q_buf[h] = part
            else:
                kv_own[j - 1, h] = part

    far_copies = []
    turns = []

    def describe(src, dst, send_at, recv_at, peer):
        return pltpu.make_async_remote_copy(
            src_ref=src, dst_ref=dst, send_sem=send_sem.at[send_at], recv_sem=recv_sem.at[recv_at],
            device_id=peer, device_id_type=MESH,
        )

    sides = ((0, after, 3, z_up, y_up), (1, before, 0, z_down, y_down))
    turned = ((0, 0, 2), (1, 0, 2), (1, 2, 3))
    for slot, (kv, first, count) in enumerate(turned):
        some_heads = pl.ds(first, count)
        for side, peer, last, z_next, y_next in sides:
            source, place = kv_own.at[kv, some_heads, halves[side]], kv_far.at[side, kv, some_heads]
            at, turn_at = len(copies), N_COPIES - 1 - slot
            staged = turning.at[pl.ds((0, 2, 4)[slot], count)]
            straight = describe(source, place, at, at, peer)
            turn = describe(source, staged, at, turn_at, z_next)
            onward = describe(staged, place, turn_at, at, y_next)
            copies.append(straight)
            far_copies.append(straight)
            turns.append((last, straight, turn, onward))

            @pl.when(y == last)
            def _():
                turn.start()

    def send_straight():
        for last, straight, _, _ in turns:

            @pl.when(y != last)
            def _():
                straight.start()

        for side, peer, _, _, _ in sides:
            source, place = kv_own.at[0, pl.ds(2, 3), halves[side]], kv_far.at[side, 0, pl.ds(2, 3)]
            far_copies.append(remote(source, place, peer))

    def pass_turned():
        for last, _, turn, onward in turns:

            @pl.when(y == last)
            def _():
                turn.wait_recv()
                onward.start()

    ones = jnp.ones((BLOCK, HD), bf16)
    everything = pl.ds(0, rows)

    def weigh(h, at, scores, count, first=False):
        pieces = [scores[:, i * BLOCK : (i + 1) * BLOCK] for i in range(count)]
        top = functools.reduce(jnp.maximum, pieces)
        top = jnp.broadcast_to(jnp.max(top, axis=1, keepdims=True), pieces[0].shape)
        keep = None
        if not first:
            old = m_buf[h, at]
            top = jnp.maximum(top, old)
            keep = jnp.exp2((old - top) * SCALE)
        m_buf[h, at] = top
        scaled = top * SCALE
        return [jnp.exp2(piece * SCALE - scaled) for piece in pieces], keep

    def mix(pieces, values):
        weight = jnp.concatenate([piece.astype(bf16) for piece in pieces], axis=1)
        values = jnp.concatenate([values, jnp.concatenate([ones] * len(pieces), axis=0)], axis=1)
        return jnp.dot(weight, values, preferred_element_type=f32)

    def attend(h, at, scores, values, count, first=False):
        pieces, keep = weigh(h, at, scores, count, first)
        mixed = mix(pieces, values)
        for side in range(2):
            lanes = pl.ds(side * HD, HD)
            part = mixed[:, side * HD : (side + 1) * HD]
            acc_buf[h, at, lanes] = part if first else acc_buf[h, at, lanes] * keep + part

    contract = (((1,), (1,)), ((), ()))

    def slot_scores(places):
        first_lane = lax.broadcasted_iota(jnp.int32, (BLOCK, HD), 1) == 0
        bias = []
        for back, position in places:
            holder = ((z + 4 - back) % 4) * 4 + (y + 4 - COLUMN[position]) % 4
            _, found = wanted(holder, sp)
            low = jnp.where(found > 0, 0.0, LOW).astype(f32)
            bias.append(jnp.where(first_lane, low, 0.0).astype(bf16))
        bias = jnp.concatenate(bias, axis=0)
        pointer = jnp.where(lax.broadcasted_iota(jnp.int32, (rows, HD), 1) == 0, 1.0, 0.0).astype(bf16)
        for h in range(heads):
            keys = slot_rows(0, h, places)
            yield h, lax.dot_general(
                jnp.concatenate([q_buf[h], pointer], axis=1),
                jnp.concatenate([keys, bias], axis=1),
                contract,
                preferred_element_type=f32,
            )

    def slot_rows(kv, h, places):
        return jnp.concatenate([row[kv, b, p, :, pl.ds(h * HD, HD)] for b, p in places], axis=0)

    def slots(places):
        for h, scores in slot_scores(places):
            attend(h, everything, scores, slot_rows(1, h, places), len(places))

    def rows_of(part, bias, first=False):
        for h in range(heads):
            scores = lax.dot_general(q_buf[h], part(0, h), contract, preferred_element_type=f32)
            attend(h, pl.ds(0, rows), scores + bias[...], part(1, h), 4, first)

    near_spread.near[2].wait_recv()
    project(tok_near, 0, 1, True)
    rows_of(lambda kv, h: kv_own[kv, h], bias_own, first=True)
    for copy in z_copies[0, 0] + z_copies[1, 0]:
        copy.wait_recv()
    y_pass(1)
    z_send(1, 1, 2)
    send_straight()
    slots(((0, 0), (0, 1), (0, 2), (1, 0), (2, 0), (3, 0)))

    near_spread.pass_near()
    for back in (1, 3):
        near_spread.near_sibling[back].wait_recv()
        project(tok_near, back, 1, False)
    for copy in y_far[0]:
        copy.wait_recv()
    z_send(0, 3, 1)
    pass_turned()
    near_spread.pass_far()
    for copy in y_far[1]:
        copy.wait_recv()
    z_send(1, 3, 1)
    for copy in near_spread.far_sibling:
        copy.wait_recv()
    project(tok_near, 2, 1, False)
    tok[0] = total[:, : 2 * width].astype(bf16)
    rows_of(lambda kv, h: tok[0, :, pl.ds(kv * width + h * HD, HD)], bias_near)
    for copy in z_copies[0, 1] + z_copies[1, 1]:
        copy.wait_recv()
    slots(((1, 1), (1, 2), (2, 1), (2, 2), (3, 1), (3, 2), (0, 3)))

    for copy in far_copies:
        copy.wait_recv()
    for h in range(heads):
        for side in range(2):
            at = halves[side]
            scores = lax.dot_general(q_buf[h, at], kv_far[side, 0, h], contract, preferred_element_type=f32)
            attend(h, at, scores + bias_far[side], kv_far[side, 1, h], 2)

    last_places = ((1, 3), (2, 3), (3, 3))
    span = len(last_places) * BLOCK
    for copy in z_copies[0, 3]:
        copy.wait_recv()
    for h, scores in slot_scores(last_places):
        pieces, keep = weigh(h, everything, scores, len(last_places))
        for i, piece in enumerate(pieces):
            total[:, pl.ds(h * span + i * BLOCK, BLOCK)] = piece
        for side in range(2):
            lanes = pl.ds(side * HD, HD)
            acc_buf[h, :, lanes] = acc_buf[h, :, lanes] * keep
    for copy in z_copies[1, 3]:
        copy.wait_recv()
    out_copies = []
    for h in range(heads):
        pieces = [total[:, pl.ds(h * span + i * BLOCK, BLOCK)] for i in range(len(last_places))]
        sums = acc_buf[h] + mix(pieces, slot_rows(1, h, last_places))
        lanes = pl.ds(h * HD, HD)
        q_buf[h] = (sums[:, :HD] / sums[:, HD:]).astype(out.dtype)
        out_copies.append(pltpu.make_async_copy(q_buf.at[h], out.at[:, lanes], out_sem.at[h]))
        out_copies[h].start()
    for copy in out_copies:
        copy.wait()

    assert len(copies) <= N_COPIES - 3
    for copy in copies:
        copy.wait_send()
    for last, _, _, onward in turns:

        @pl.when(y == last)
        def _():
            onward.wait_send()


def body(tokens, w_query, w_key, w_value, cache_keys, cache_values, tile_level, window_map):
    rows, width = tokens.shape
    heads = width // HD
    bf16, f32 = jnp.bfloat16, jnp.float32
    block = (BLOCK, width)
    return pl.pallas_call(
        kernel,
        out_shape=jax.ShapeDtypeStruct((rows, width), bf16),
        in_specs=[pl.BlockSpec(memory_space=pl.ANY)] * 6 + [pl.BlockSpec(memory_space=pltpu.SMEM)] * 2,
        out_specs=pl.BlockSpec(memory_space=pl.ANY),
        scratch_shapes=[
            pltpu.VMEM((4, rows, 2 * width), bf16),
            pltpu.VMEM((4, rows, 2 * width), bf16),
            pltpu.VMEM((4, 2 * width, 3 * width), bf16),
            pltpu.VMEM((rows, 3 * width), f32),
            pltpu.VMEM((heads, rows, HD), bf16),
            pltpu.VMEM((2, heads, rows, HD), bf16),
            pltpu.VMEM((2, 2, heads, rows // 2, HD), bf16),
            pltpu.VMEM((4,) + block, bf16),
            pltpu.VMEM((4,) + block, bf16),
            pltpu.VMEM((4,) + block, bf16),
            pltpu.VMEM((4,) + block, bf16),
            pltpu.VMEM((4,) + block, bf16),
            pltpu.VMEM((4,) + block, bf16),
            pltpu.VMEM((4,) + block, bf16),
            pltpu.VMEM((4,) + block, bf16),
            pltpu.VMEM((2, 3, 4) + block, bf16),
            pltpu.VMEM((2, 4, 4) + block, bf16),
            pltpu.VMEM((heads, rows, HD), f32),
            pltpu.VMEM((heads, rows, 2 * HD), f32),
            pltpu.VMEM((rows, rows), f32),
            pltpu.VMEM((rows, rows), f32),
            pltpu.VMEM((2, rows // 2, rows // 2), f32),
            pltpu.VMEM((7, rows // 2, HD), bf16),
            pltpu.SemaphoreType.DMA((4, 3)),
            pltpu.SemaphoreType.DMA((3,)),
            pltpu.SemaphoreType.DMA((heads,)),
            pltpu.SemaphoreType.DMA((N_COPIES,)),
            pltpu.SemaphoreType.DMA((N_COPIES,)),
        ],
        compiler_params=pltpu.CompilerParams(
            collective_id=0, has_side_effects=True, vmem_limit_bytes=63 * 1024 * 1024
        ),
    )(tokens, w_query, w_key, w_value, cache_keys, cache_values, tile_level, window_map.T)


def solution(mesh):
    placed = (
        P("sp", "tp"),
        P(None, "tp"),
        P(None, "tp"),
        P(None, "tp"),
        P("sp", None, "tp"),
        P("sp", None, "tp"),
        P("sp"),
        P(),
    )
    return jax.shard_map(body, mesh=mesh, in_specs=placed, out_specs=P("sp", "tp"), check_vma=False)
```

```python
import functools
import math

import jax
import jax.numpy as jnp
from jax import lax
from jax.experimental import pallas as pl
from jax.experimental.pallas import tpu as pltpu
from jax.sharding import PartitionSpec as P

HD = 128
TILE = 128
BLOCK = 128
MESH = pl.DeviceIdType.MESH
LOW = -1e30
SCALE = math.log2(math.e) / math.sqrt(HD)
COLUMN = (0, 1, 3, 2)
N_COPIES = 60


def kernel(
    tokens, w_query, w_key, w_value, cache_keys, cache_values, tile_level, window_map,
    out,
    tok, tok_near, weights, total, q_buf, kv_own, kv_far, k_0, k_1, k_2, k_3, v_0, v_1, v_2, v_3, send, row,
    m_buf, acc_buf, bias_own, bias_near, bias_far, turning,
    weight_sem, local_sem, out_sem, send_sem, recv_sem,
):
    sp = lax.axis_index("sp")
    tp = lax.axis_index("tp")
    z, y = sp // 4, sp % 4
    x, core = tp // 2, tp % 2
    rows, width = tokens.shape
    heads = width // HD
    half = rows // 2
    f32, bf16 = jnp.float32, jnp.bfloat16

    sibling = (sp, x * 2 + 1 - core)
    x_up = (sp, ((x + 1) % 4) * 2 + core)
    x_down = (sp, ((x + 3) % 4) * 2 + core)
    y_up = (z * 4 + (y + 1) % 4, tp)
    y_down = (z * 4 + (y + 3) % 4, tp)
    z_up = (((z + 1) % 4) * 4 + y, tp)
    z_down = (((z + 3) % 4) * 4 + y, tp)
    z_far = (((z + 2) % 4) * 4 + y, tp)
    after = ((sp + 1) % 16, tp)
    before = ((sp + 15) % 16, tp)
    held = ((k_0, v_0), (k_1, v_1), (k_2, v_2), (k_3, v_3))
    peers = (sibling, x_up, x_down, y_up, y_down, z_up, z_down, z_far)
    has_after, has_before = sp < 15, sp > 0
    far_after, far_before = has_after & (y == 3), has_before & (y == 0)

    barrier = pltpu.get_barrier_semaphore()
    for peer in peers:
        pl.semaphore_signal(barrier, inc=1, device_id=peer, device_id_type=MESH)
    for far, peer in ((far_after, after), (far_before, before)):

        @pl.when(far)
        def _():
            pl.semaphore_signal(barrier, inc=1, device_id=peer, device_id_type=MESH)

    lane = pl.ds(pl.multiple_of(core * width, HD), width)
    own_tokens = pltpu.make_async_copy(tokens, tok.at[0, :, lane], local_sem.at[0])
    own_blocks = [
        pltpu.make_async_copy(cache, held[0][kv], local_sem.at[1 + kv])
        for kv, cache in enumerate((cache_keys, cache_values))
    ]
    own_blocks[0].start()
    own_blocks[1].start()
    own_tokens.start()
    pl.semaphore_wait(barrier, len(peers) + far_after.astype(jnp.int32) + far_before.astype(jnp.int32))

    copies = []

    def describe(src, dst, send_at, recv_at, peer):
        return pltpu.make_async_remote_copy(
            src_ref=src, dst_ref=dst, send_sem=send_sem.at[send_at], recv_sem=recv_sem.at[recv_at],
            device_id=peer, device_id_type=MESH,
        )

    def remote(src, dst, peer):
        at = len(copies)
        copy = describe(src, dst, at, at, peer)
        copy.start()
        copies.append((None, copy))
        return copy

    sent = (has_after, has_before)
    received = (has_before, has_after)

    def prepare(src, dst, side):
        at = len(copies)
        copy = describe(src, dst, at, at, (after, before)[side])
        copies.append((sent[side], copy))
        return copy

    def start_where(condition, copy):
        @pl.when(condition)
        def _():
            copy.start()

    def wait_for_side(side, copy):
        @pl.when(received[side])
        def _():
            copy.wait_recv()

    halves = (pl.ds(0, half), pl.ds(half, half))

    class Spread:
        def __init__(self, buf, source):
            self.buf = buf
            self.near = [
                remote(source, buf.at[1, :, lane], x_up),
                remote(source, buf.at[3, :, lane], x_down),
                remote(source, buf.at[0, :, lane], sibling),
            ]

        def pass_near(self):
            buf = self.buf
            self.far = []
            for part, back, peer in ((0, 1, x_up), (1, 3, x_down)):
                self.near[part].wait_recv()
                piece = halves[part]
                self.far.append(remote(buf.at[back, piece, lane], buf.at[2, piece, lane], peer))
            self.near_sibling = {
                back: remote(buf.at[back, :, lane], buf.at[back, :, lane], sibling) for back in (1, 3)
            }

        def pass_far(self):
            buf = self.buf
            self.far_sibling = []
            for part in range(2):
                self.far[part].wait_recv()
                piece = halves[part]
                self.far_sibling.append(remote(buf.at[2, piece, lane], buf.at[2, piece, lane], sibling))

    y_near = {0: [remote(cache_keys, held[1][0], y_up), remote(cache_keys, held[3][0], y_down)]}
    own_spread = Spread(tok, tokens)
    near_tokens = [
        prepare(tokens.at[halves[1 - side], :], tok_near.at[0, halves[side], lane], side) for side in range(2)
    ]
    for side in range(2):
        start_where(sent[side], near_tokens[side])
    y_near[1] = [remote(cache_values, held[1][1], y_up), remote(cache_values, held[3][1], y_down)]

    depth = 2 * width
    weight_copies = {}
    for back in (0, 1, 3, 2):
        source = pl.ds(pl.multiple_of(((x + 4 - back) % 4) * depth, depth), depth)
        for j, w in enumerate((w_query, w_key, w_value)):
            copy = pltpu.make_async_copy(
                w.at[source, :], weights.at[back, :, pl.ds(j * width, width)], weight_sem.at[back, j]
            )
            copy.start()
            weight_copies[back, j] = copy

    def wanted(holder, owner):
        local, found = jnp.int32(0), jnp.int32(0)
        for k in range(8):
            block = window_map[k, owner]
            hit = jnp.where(block // 4 == holder, 1, 0)
            local = local + hit * (block % 4)
            found = found + hit
        return local, found

    z_copies = {}

    def z_send(kv, first, count):
        for position in range(first, first + count):
            column = COLUMN[position]
            holder = z * 4 + (y + 4 - column) % 4
            for step in range(4):
                local, _ = wanted(holder, ((z + step) % 4) * 4 + y)
                block = held[column][kv][local]
                if step == 0:
                    row[kv, 0, position] = block
                else:
                    send[kv, step - 1, position] = block
        slots = pl.ds(first, count)
        z_copies[kv, first] = [
            remote(send.at[kv, 1, slots], row.at[kv, 2, slots], z_far),
            remote(send.at[kv, 0, slots], row.at[kv, 1, slots], z_up),
            remote(send.at[kv, 2, slots], row.at[kv, 3, slots], z_down),
        ]

    y_far = {}

    def y_pass(kv):
        low, high = pl.ds(0, 2), pl.ds(2, 2)
        for copy in y_near[kv]:
            copy.wait_recv()
        y_far[kv] = [
            remote(held[1][kv].at[low], held[2][kv].at[low], y_up),
            remote(held[3][kv].at[high], held[2][kv].at[high], y_down),
        ]

    def project(buf, back, first, start):
        wide = (3 - first) * width
        for at in range(0, wide, 2 * HD):
            columns = pl.ds(at, min(2 * HD, wide - at))
            source = pl.ds(first * width + at, min(2 * HD, wide - at))
            product = jnp.dot(buf[back], weights[back, :, source], preferred_element_type=f32)
            if start:
                total[:, columns] = product
            else:
                total[:, columns] += product

    def project_own(back, start=False):
        for j in range(3):
            weight_copies[back, j].wait()
        project(tok, back, 0, start)

    for side in range(2):

        @pl.when(jnp.logical_not(received[side]))
        def _():
            tok_near[0, halves[side], lane] = jnp.zeros((half, width), bf16)
            kv_far[side] = jnp.zeros_like(kv_far[side])

    for kv in range(2):
        own_blocks[kv].wait()
        z_send(kv, 0, 1)

    own_tokens.wait()
    own_spread.near[2].wait_recv()
    project_own(0, True)

    def radius_of(first, count):
        at = lax.broadcasted_iota(jnp.int32, (count, 1), 0) + first
        radius = jnp.zeros((count, 1), jnp.int32)
        for tile in range(rows // TILE):
            radius = jnp.where(at // TILE == tile, (tile_level[tile] + 1) * rows // 3, radius)
        return radius, at

    def bias_of(first, count, key_first, key_count, exists):
        radius, at = radius_of(first, count)
        key_at = lax.broadcasted_iota(jnp.int32, (count, key_count), 1) + key_first
        allowed = jnp.abs(key_at - at) <= radius
        if exists is not None:
            allowed = allowed & exists
        return jnp.where(allowed, 0.0, LOW).astype(f32)

    for part in range(2):
        first = part * half
        bias_own[halves[part], :] = bias_of(first, half, 0, rows, None)
        bias_near[halves[part], halves[0]] = bias_of(first, half, -half, half, sp > 0)
        bias_near[halves[part], halves[1]] = bias_of(first, half, rows, half, sp < 15)
    bias_far[0] = bias_of(0, half, -rows, half, sp > 0)
    bias_far[1] = bias_of(half, half, rows + half, half, sp < 15)

    own_spread.pass_near()
    y_pass(0)
    z_send(0, 1, 2)

    for back in (1, 3):
        own_spread.near_sibling[back].wait_recv()
        project_own(back)
    own_spread.pass_far()
    for side in range(2):
        wait_for_side(side, near_tokens[side])
    near_spread = Spread(tok_near, tok_near.at[0, :, lane])
    for copy in own_spread.far_sibling:
        copy.wait_recv()
    project_own(2)

    for h in range(heads):
        for j in range(3):
            part = total[:, pl.ds(j * width + h * HD, HD)].astype(bf16)
            if j == 0:
                q_buf[h] = part
            else:
                kv_own[j - 1, h] = part

    far_copies = []
    turns = []
    last_ones = ((y == 3, z_up, y_up, z > 0), (y == 0, z_down, y_down, z < 3))
    turned = ((0, 0, 2), (1, 0, 2), (1, 2, 3))
    for slot, (kv, first, count) in enumerate(turned):
        some_heads = pl.ds(first, count)
        for side in range(2):
            last, z_next, y_next, comes = last_ones[side]
            source, place = kv_own.at[kv, some_heads, halves[side]], kv_far.at[side, kv, some_heads]
            at, turn_at = len(copies), N_COPIES - 1 - slot
            staged = turning.at[pl.ds((0, 2, 4)[slot], count)]
            straight = prepare(source, place, side)
            far_copies.append((side, straight))
            turn = describe(source, staged, at, turn_at, z_next)
            onward = describe(staged, place, turn_at, at, y_next)
            turns.append((sent[side] & jnp.logical_not(last), straight, last & comes, turn, onward))
            start_where(sent[side] & last, turn)

    def send_straight():
        for here, straight, _, _, _ in turns:
            start_where(here, straight)
        for side in range(2):
            copy = prepare(kv_own.at[0, pl.ds(2, 3), halves[side]], kv_far.at[side, 0, pl.ds(2, 3)], side)
            far_copies.append((side, copy))
            start_where(sent[side], copy)

    def pass_turned():
        for _, _, here, turn, onward in turns:

            @pl.when(here)
            def _():
                turn.wait_recv()
                onward.start()

    ones = jnp.ones((BLOCK, HD), bf16)
    everything = pl.ds(0, rows)

    def weigh(h, at, scores, count, first=False):
        pieces = [scores[:, i * BLOCK : (i + 1) * BLOCK] for i in range(count)]
        top = functools.reduce(jnp.maximum, pieces)
        top = jnp.broadcast_to(jnp.max(top, axis=1, keepdims=True), pieces[0].shape)
        keep = None
        if not first:
            old = m_buf[h, at]
            top = jnp.maximum(top, old)
            keep = jnp.exp2((old - top) * SCALE)
        m_buf[h, at] = top
        scaled = top * SCALE
        return [jnp.exp2(piece * SCALE - scaled) for piece in pieces], keep

    def mix(pieces, values):
        weight = jnp.concatenate([piece.astype(bf16) for piece in pieces], axis=1)
        values = jnp.concatenate([values, jnp.concatenate([ones] * len(pieces), axis=0)], axis=1)
        return jnp.dot(weight, values, preferred_element_type=f32)

    def attend(h, at, scores, values, count, first=False):
        pieces, keep = weigh(h, at, scores, count, first)
        mixed = mix(pieces, values)
        for side in range(2):
            lanes = pl.ds(side * HD, HD)
            part = mixed[:, side * HD : (side + 1) * HD]
            acc_buf[h, at, lanes] = part if first else acc_buf[h, at, lanes] * keep + part

    contract = (((1,), (1,)), ((), ()))

    def slot_scores(places):
        first_lane = lax.broadcasted_iota(jnp.int32, (BLOCK, HD), 1) == 0
        bias = []
        for back, position in places:
            holder = ((z + 4 - back) % 4) * 4 + (y + 4 - COLUMN[position]) % 4
            _, found = wanted(holder, sp)
            low = jnp.where(found > 0, 0.0, LOW).astype(f32)
            bias.append(jnp.where(first_lane, low, 0.0).astype(bf16))
        bias = jnp.concatenate(bias, axis=0)
        pointer = jnp.where(lax.broadcasted_iota(jnp.int32, (rows, HD), 1) == 0, 1.0, 0.0).astype(bf16)
        for h in range(heads):
            keys = slot_rows(0, h, places)
            yield h, lax.dot_general(
                jnp.concatenate([q_buf[h], pointer], axis=1),
                jnp.concatenate([keys, bias], axis=1),
                contract,
                preferred_element_type=f32,
            )

    def slot_rows(kv, h, places):
        return jnp.concatenate([row[kv, b, p, :, pl.ds(h * HD, HD)] for b, p in places], axis=0)

    def slots(places):
        for h, scores in slot_scores(places):
            attend(h, everything, scores, slot_rows(1, h, places), len(places))

    def rows_of(part, bias, first=False):
        for h in range(heads):
            scores = lax.dot_general(q_buf[h], part(0, h), contract, preferred_element_type=f32)
            attend(h, pl.ds(0, rows), scores + bias[...], part(1, h), 4, first)

    near_spread.near[2].wait_recv()
    project(tok_near, 0, 1, True)
    rows_of(lambda kv, h: kv_own[kv, h], bias_own, first=True)
    for copy in z_copies[0, 0] + z_copies[1, 0]:
        copy.wait_recv()
    y_pass(1)
    z_send(1, 1, 2)
    send_straight()
    slots(((0, 0), (0, 1), (0, 2), (1, 0), (2, 0), (3, 0)))

    near_spread.pass_near()
    for back in (1, 3):
        near_spread.near_sibling[back].wait_recv()
        project(tok_near, back, 1, False)
    for copy in y_far[0]:
        copy.wait_recv()
    z_send(0, 3, 1)
    pass_turned()
    near_spread.pass_far()
    for copy in y_far[1]:
        copy.wait_recv()
    z_send(1, 3, 1)
    for copy in near_spread.far_sibling:
        copy.wait_recv()
    project(tok_near, 2, 1, False)
    tok[0] = total[:, : 2 * width].astype(bf16)
    rows_of(lambda kv, h: tok[0, :, pl.ds(kv * width + h * HD, HD)], bias_near)
    for copy in z_copies[0, 1] + z_copies[1, 1]:
        copy.wait_recv()
    slots(((1, 1), (1, 2), (2, 1), (2, 2), (3, 1), (3, 2), (0, 3)))

    for side, copy in far_copies:
        wait_for_side(side, copy)
    for h in range(heads):
        for side in range(2):
            at = halves[side]
            scores = lax.dot_general(q_buf[h, at], kv_far[side, 0, h], contract, preferred_element_type=f32)
            attend(h, at, scores + bias_far[side], kv_far[side, 1, h], 2)

    last_places = ((1, 3), (2, 3), (3, 3))
    span = len(last_places) * BLOCK
    for copy in z_copies[0, 3]:
        copy.wait_recv()
    for h, scores in slot_scores(last_places):
        pieces, keep = weigh(h, everything, scores, len(last_places))
        for i, piece in enumerate(pieces):
            total[:, pl.ds(h * span + i * BLOCK, BLOCK)] = piece
        for side in range(2):
            lanes = pl.ds(side * HD, HD)
            acc_buf[h, :, lanes] = acc_buf[h, :, lanes] * keep
    for copy in z_copies[1, 3]:
        copy.wait_recv()
    out_copies = []
    for h in range(heads):
        pieces = [total[:, pl.ds(h * span + i * BLOCK, BLOCK)] for i in range(len(last_places))]
        sums = acc_buf[h] + mix(pieces, slot_rows(1, h, last_places))
        lanes = pl.ds(h * HD, HD)
        q_buf[h] = (sums[:, :HD] / sums[:, HD:]).astype(out.dtype)
        out_copies.append(pltpu.make_async_copy(q_buf.at[h], out.at[:, lanes], out_sem.at[h]))
        out_copies[h].start()
    for copy in out_copies:
        copy.wait()

    assert len(copies) <= N_COPIES - 3
    for condition, copy in copies:
        if condition is None:
            copy.wait_send()
        else:

            @pl.when(condition)
            def _():
                copy.wait_send()

    for _, _, here, _, onward in turns:

        @pl.when(here)
        def _():
            onward.wait_send()


def body(tokens, w_query, w_key, w_value, cache_keys, cache_values, tile_level, window_map):
    rows, width = tokens.shape
    heads = width // HD
    bf16, f32 = jnp.bfloat16, jnp.float32
    block = (BLOCK, width)
    return pl.pallas_call(
        kernel,
        out_shape=jax.ShapeDtypeStruct((rows, width), bf16),
        in_specs=[pl.BlockSpec(memory_space=pl.ANY)] * 6 + [pl.BlockSpec(memory_space=pltpu.SMEM)] * 2,
        out_specs=pl.BlockSpec(memory_space=pl.ANY),
        scratch_shapes=[
            pltpu.VMEM((4, rows, 2 * width), bf16),
            pltpu.VMEM((4, rows, 2 * width), bf16),
            pltpu.VMEM((4, 2 * width, 3 * width), bf16),
            pltpu.VMEM((rows, 3 * width), f32),
            pltpu.VMEM((heads, rows, HD), bf16),
            pltpu.VMEM((2, heads, rows, HD), bf16),
            pltpu.VMEM((2, 2, heads, rows // 2, HD), bf16),
            pltpu.VMEM((4,) + block, bf16),
            pltpu.VMEM((4,) + block, bf16),
            pltpu.VMEM((4,) + block, bf16),
            pltpu.VMEM((4,) + block, bf16),
            pltpu.VMEM((4,) + block, bf16),
            pltpu.VMEM((4,) + block, bf16),
            pltpu.VMEM((4,) + block, bf16),
            pltpu.VMEM((4,) + block, bf16),
            pltpu.VMEM((2, 3, 4) + block, bf16),
            pltpu.VMEM((2, 4, 4) + block, bf16),
            pltpu.VMEM((heads, rows, HD), f32),
            pltpu.VMEM((heads, rows, 2 * HD), f32),
            pltpu.VMEM((rows, rows), f32),
            pltpu.VMEM((rows, rows), f32),
            pltpu.VMEM((2, rows // 2, rows // 2), f32),
            pltpu.VMEM((7, rows // 2, HD), bf16),
            pltpu.SemaphoreType.DMA((4, 3)),
            pltpu.SemaphoreType.DMA((3,)),
            pltpu.SemaphoreType.DMA((heads,)),
            pltpu.SemaphoreType.DMA((N_COPIES,)),
            pltpu.SemaphoreType.DMA((N_COPIES,)),
        ],
        compiler_params=pltpu.CompilerParams(
            collective_id=0, has_side_effects=True, vmem_limit_bytes=63 * 1024 * 1024
        ),
    )(tokens, w_query, w_key, w_value, cache_keys, cache_values, tile_level, window_map.T)


def solution(mesh):
    placed = (
        P("sp", "tp"),
        P(None, "tp"),
        P(None, "tp"),
        P(None, "tp"),
        P("sp", None, "tp"),
        P("sp", None, "tp"),
        P("sp"),
        P(),
    )
    return jax.shard_map(body, mesh=mesh, in_specs=placed, out_specs=P("sp", "tp"), check_vma=False)
```

```python
import functools
import math

import jax
import jax.numpy as jnp
from jax import lax
from jax.experimental import pallas as pl
from jax.experimental.pallas import tpu as pltpu
from jax.sharding import PartitionSpec as P

HD = 128
TILE = 128
BLOCK = 128
MESH = pl.DeviceIdType.MESH
LOW = -1e30
SCALE = math.log2(math.e) / math.sqrt(HD)
COLUMN = (0, 1, 3, 2)
N_COPIES = 66


def kernel(
    tokens, w_query, w_key, w_value, cache_keys, cache_values, tile_level, window_map,
    out,
    tok, tok_near, weights, total, q_buf, kv_own, kv_far, k_0, k_1, k_2, k_3, k_1b, k_3b, v_0, v_1, v_2, v_3, send, row,
    m_buf, acc_buf, bias_own, bias_near, bias_far, turning,
    weight_sem, local_sem, out_sem, send_sem, recv_sem,
):
    sp = lax.axis_index("sp")
    tp = lax.axis_index("tp")
    z, y = sp // 4, sp % 4
    x, core = tp // 2, tp % 2
    rows, width = tokens.shape
    heads = width // HD
    half = rows // 2
    f32, bf16 = jnp.float32, jnp.bfloat16

    sibling = (sp, x * 2 + 1 - core)
    x_up = (sp, ((x + 1) % 4) * 2 + core)
    x_down = (sp, ((x + 3) % 4) * 2 + core)
    y_up = (z * 4 + (y + 1) % 4, tp)
    y_down = (z * 4 + (y + 3) % 4, tp)
    z_up = (((z + 1) % 4) * 4 + y, tp)
    z_down = (((z + 3) % 4) * 4 + y, tp)
    z_far = (((z + 2) % 4) * 4 + y, tp)
    after = ((sp + 1) % 16, tp)
    before = ((sp + 15) % 16, tp)
    held = ((k_0, v_0), (k_1, v_1), (k_2, v_2), (k_3, v_3))
    cuts = (pl.ds(0, 3 * HD), pl.ds(3 * HD, width - 3 * HD))
    cut_keys = {1: (k_1, k_1b), 3: (k_3, k_3b)}
    peers = (sibling, x_up, x_down, y_up, y_down, z_up, z_down, z_far)
    has_after, has_before = sp < 15, sp > 0
    far_after, far_before = has_after & (y == 3), has_before & (y == 0)

    barrier = pltpu.get_barrier_semaphore()
    for peer in peers:
        pl.semaphore_signal(barrier, inc=1, device_id=peer, device_id_type=MESH)
    for far, peer in ((far_after, after), (far_before, before)):

        @pl.when(far)
        def _():
            pl.semaphore_signal(barrier, inc=1, device_id=peer, device_id_type=MESH)

    lane = pl.ds(pl.multiple_of(core * width, HD), width)
    own_tokens = pltpu.make_async_copy(tokens, tok.at[0, :, lane], local_sem.at[0])
    own_blocks = [
        pltpu.make_async_copy(cache, held[0][kv], local_sem.at[1 + kv])
        for kv, cache in enumerate((cache_keys, cache_values))
    ]
    own_blocks[0].start()
    own_blocks[1].start()
    own_tokens.start()
    pl.semaphore_wait(barrier, len(peers) + far_after.astype(jnp.int32) + far_before.astype(jnp.int32))

    copies = []

    def describe(src, dst, send_at, recv_at, peer):
        return pltpu.make_async_remote_copy(
            src_ref=src, dst_ref=dst, send_sem=send_sem.at[send_at], recv_sem=recv_sem.at[recv_at],
            device_id=peer, device_id_type=MESH,
        )

    def remote(src, dst, peer):
        at = len(copies)
        copy = describe(src, dst, at, at, peer)
        copy.start()
        copies.append((None, copy))
        return copy

    sent = (has_after, has_before)
    received = (has_before, has_after)

    def prepare(src, dst, side):
        at = len(copies)
        copy = describe(src, dst, at, at, (after, before)[side])
        copies.append((sent[side], copy))
        return copy

    def start_where(condition, copy):
        @pl.when(condition)
        def _():
            copy.start()

    def wait_for_side(side, copy):
        @pl.when(received[side])
        def _():
            copy.wait_recv()

    halves = (pl.ds(0, half), pl.ds(half, half))

    class Spread:
        def __init__(self, buf, source):
            self.buf = buf
            self.near = [
                remote(source, buf.at[1, :, lane], x_up),
                remote(source, buf.at[3, :, lane], x_down),
                remote(source, buf.at[0, :, lane], sibling),
            ]

        def pass_near(self):
            buf = self.buf
            self.far = []
            for part, back, peer in ((0, 1, x_up), (1, 3, x_down)):
                self.near[part].wait_recv()
                piece = halves[part]
                self.far.append(remote(buf.at[back, piece, lane], buf.at[2, piece, lane], peer))
            self.near_sibling = {
                back: remote(buf.at[back, :, lane], buf.at[back, :, lane], sibling) for back in (1, 3)
            }

        def pass_far(self):
            buf = self.buf
            self.far_sibling = []
            for part in range(2):
                self.far[part].wait_recv()
                piece = halves[part]
                self.far_sibling.append(remote(buf.at[2, piece, lane], buf.at[2, piece, lane], sibling))

    y_near = {}
    near_keys = []
    for part in range(2):
        source = cache_keys.at[:, :, cuts[part]]
        near_keys.append([remote(source, cut_keys[1][part], y_up), remote(source, cut_keys[3][part], y_down)])
        if part == 0:
            own_spread = Spread(tok, tokens)
    near_tokens = [
        prepare(tokens.at[halves[1 - side], :], tok_near.at[0, halves[side], lane], side) for side in range(2)
    ]
    for side in range(2):
        start_where(sent[side], near_tokens[side])
    y_near[1] = [remote(cache_values, held[1][1], y_up), remote(cache_values, held[3][1], y_down)]

    depth = 2 * width
    weight_copies = {}
    for back in (0, 1, 3, 2):
        source = pl.ds(pl.multiple_of(((x + 4 - back) % 4) * depth, depth), depth)
        for j, w in enumerate((w_query, w_key, w_value)):
            copy = pltpu.make_async_copy(
                w.at[source, :], weights.at[back, :, pl.ds(j * width, width)], weight_sem.at[back, j]
            )
            copy.start()
            weight_copies[back, j] = copy

    def wanted(holder, owner):
        local, found = jnp.int32(0), jnp.int32(0)
        for k in range(8):
            block = window_map[k, owner]
            hit = jnp.where(block // 4 == holder, 1, 0)
            local = local + hit * (block % 4)
            found = found + hit
        return local, found

    z_copies = {}

    def z_send(kv, first, count):
        for position in range(first, first + count):
            column = COLUMN[position]
            holder = z * 4 + (y + 4 - column) % 4
            for step in range(4):
                local, _ = wanted(holder, ((z + step) % 4) * 4 + y)
                block = held[column][kv][local]
                if step == 0:
                    row[kv, 0, position] = block
                else:
                    send[kv, step - 1, position] = block
        slots = pl.ds(first, count)
        z_copies[kv, first] = [
            remote(send.at[kv, 1, slots], row.at[kv, 2, slots], z_far),
            remote(send.at[kv, 0, slots], row.at[kv, 1, slots], z_up),
            remote(send.at[kv, 2, slots], row.at[kv, 3, slots], z_down),
        ]

    y_far = {}

    def pass_keys(part):
        cut = cuts[part]
        for copy in near_keys[part]:
            copy.wait_recv()
        low, high = pl.ds(0, 2), pl.ds(2, 2)
        y_far.setdefault(0, []).extend([
            remote(cut_keys[1][part].at[low], held[2][0].at[low, :, cut], y_up),
            remote(cut_keys[3][part].at[high], held[2][0].at[high, :, cut], y_down),
        ])
        for position in (1, 2):
            column = COLUMN[position]
            holder = z * 4 + (y + 4 - column) % 4
            for step in range(4):
                local, _ = wanted(holder, ((z + step) % 4) * 4 + y)
                block = cut_keys[column][part][local]
                if step == 0:
                    row[0, 0, position, :, cut] = block
                else:
                    send[0, step - 1, position, :, cut] = block
        slots = pl.ds(1, 2)
        z_copies.setdefault((0, 1), []).extend([
            remote(send.at[0, 1, slots, :, cut], row.at[0, 2, slots, :, cut], z_far),
            remote(send.at[0, 0, slots, :, cut], row.at[0, 1, slots, :, cut], z_up),
            remote(send.at[0, 2, slots, :, cut], row.at[0, 3, slots, :, cut], z_down),
        ])

    def y_pass(kv):
        low, high = pl.ds(0, 2), pl.ds(2, 2)
        for copy in y_near[kv]:
            copy.wait_recv()
        y_far[kv] = [
            remote(held[1][kv].at[low], held[2][kv].at[low], y_up),
            remote(held[3][kv].at[high], held[2][kv].at[high], y_down),
        ]

    def project(buf, back, first, start):
        wide = (3 - first) * width
        for at in range(0, wide, 2 * HD):
            columns = pl.ds(at, min(2 * HD, wide - at))
            source = pl.ds(first * width + at, min(2 * HD, wide - at))
            product = jnp.dot(buf[back], weights[back, :, source], preferred_element_type=f32)
            if start:
                total[:, columns] = product
            else:
                total[:, columns] += product

    def project_own(back, start=False):
        for j in range(3):
            weight_copies[back, j].wait()
        project(tok, back, 0, start)

    for side in range(2):

        @pl.when(jnp.logical_not(received[side]))
        def _():
            tok_near[0, halves[side], lane] = jnp.zeros((half, width), bf16)
            kv_far[side] = jnp.zeros_like(kv_far[side])

    for kv in range(2):
        own_blocks[kv].wait()
        z_send(kv, 0, 1)

    own_tokens.wait()
    own_spread.near[2].wait_recv()
    project_own(0, True)

    def radius_of(first, count):
        at = lax.broadcasted_iota(jnp.int32, (count, 1), 0) + first
        radius = jnp.zeros((count, 1), jnp.int32)
        for tile in range(rows // TILE):
            radius = jnp.where(at // TILE == tile, (tile_level[tile] + 1) * rows // 3, radius)
        return radius, at

    def bias_of(first, count, key_first, key_count, exists):
        radius, at = radius_of(first, count)
        key_at = lax.broadcasted_iota(jnp.int32, (count, key_count), 1) + key_first
        allowed = jnp.abs(key_at - at) <= radius
        if exists is not None:
            allowed = allowed & exists
        return jnp.where(allowed, 0.0, LOW).astype(f32)

    for part in range(2):
        first = part * half
        bias_own[halves[part], :] = bias_of(first, half, 0, rows, None)
        bias_near[halves[part], halves[0]] = bias_of(first, half, -half, half, sp > 0)
        bias_near[halves[part], halves[1]] = bias_of(first, half, rows, half, sp < 15)
    bias_far[0] = bias_of(0, half, -rows, half, sp > 0)
    bias_far[1] = bias_of(half, half, rows + half, half, sp < 15)

    pass_keys(0)
    own_spread.pass_near()
    pass_keys(1)

    for back in (1, 3):
        own_spread.near_sibling[back].wait_recv()
        project_own(back)
    own_spread.pass_far()
    for side in range(2):
        wait_for_side(side, near_tokens[side])
    near_spread = Spread(tok_near, tok_near.at[0, :, lane])
    for copy in own_spread.far_sibling:
        copy.wait_recv()
    project_own(2)

    for h in range(heads):
        for j in range(3):
            part = total[:, pl.ds(j * width + h * HD, HD)].astype(bf16)
            if j == 0:
                q_buf[h] = part
            else:
                kv_own[j - 1, h] = part

    far_copies = []
    turns = []
    last_ones = ((y == 3, z_up, y_up, z > 0), (y == 0, z_down, y_down, z < 3))
    turned = ((0, 0, 3), (1, 0, 2), (1, 2, 3))
    for slot, (kv, first, count) in enumerate(turned):
        some_heads = pl.ds(first, count)
        for side in range(2):
            last, z_next, y_next, comes = last_ones[side]
            source, place = kv_own.at[kv, some_heads, halves[side]], kv_far.at[side, kv, some_heads]
            at, turn_at = len(copies), N_COPIES - 1 - slot
            staged = turning.at[pl.ds((0, 3, 5)[slot], count)]
            straight = prepare(source, place, side)
            far_copies.append((side, straight))
            turn = describe(source, staged, at, turn_at, z_next)
            onward = describe(staged, place, turn_at, at, y_next)
            turns.append((sent[side] & jnp.logical_not(last), straight, last & comes, turn, onward))
            start_where(sent[side] & last, turn)

    def send_straight():
        for here, straight, _, _, _ in turns:
            start_where(here, straight)
        for side in range(2):
            copy = prepare(kv_own.at[0, pl.ds(3, 2), halves[side]], kv_far.at[side, 0, pl.ds(3, 2)], side)
            far_copies.append((side, copy))
            start_where(sent[side], copy)

    def pass_turned():
        for _, _, here, turn, onward in turns:

            @pl.when(here)
            def _():
                turn.wait_recv()
                onward.start()

    ones = jnp.ones((BLOCK, HD), bf16)
    everything = pl.ds(0, rows)

    def weigh(h, at, scores, count, first=False):
        pieces = [scores[:, i * BLOCK : (i + 1) * BLOCK] for i in range(count)]
        top = functools.reduce(jnp.maximum, pieces)
        top = jnp.broadcast_to(jnp.max(top, axis=1, keepdims=True), pieces[0].shape)
        keep = None
        if not first:
            old = m_buf[h, at]
            top = jnp.maximum(top, old)
            keep = jnp.exp2((old - top) * SCALE)
        m_buf[h, at] = top
        scaled = top * SCALE
        return [jnp.exp2(piece * SCALE - scaled) for piece in pieces], keep

    def mix(pieces, values):
        weight = jnp.concatenate([piece.astype(bf16) for piece in pieces], axis=1)
        values = jnp.concatenate([values, jnp.concatenate([ones] * len(pieces), axis=0)], axis=1)
        return jnp.dot(weight, values, preferred_element_type=f32)

    def attend(h, at, scores, values, count, first=False):
        pieces, keep = weigh(h, at, scores, count, first)
        mixed = mix(pieces, values)
        for side in range(2):
            lanes = pl.ds(side * HD, HD)
            part = mixed[:, side * HD : (side + 1) * HD]
            acc_buf[h, at, lanes] = part if first else acc_buf[h, at, lanes] * keep + part

    contract = (((1,), (1,)), ((), ()))

    def slot_scores(places):
        first_lane = lax.broadcasted_iota(jnp.int32, (BLOCK, HD), 1) == 0
        bias = []
        for back, position in places:
            holder = ((z + 4 - back) % 4) * 4 + (y + 4 - COLUMN[position]) % 4
            _, found = wanted(holder, sp)
            low = jnp.where(found > 0, 0.0, LOW).astype(f32)
            bias.append(jnp.where(first_lane, low, 0.0).astype(bf16))
        bias = jnp.concatenate(bias, axis=0)
        pointer = jnp.where(lax.broadcasted_iota(jnp.int32, (rows, HD), 1) == 0, 1.0, 0.0).astype(bf16)
        for h in range(heads):
            keys = slot_rows(0, h, places)
            yield h, lax.dot_general(
                jnp.concatenate([q_buf[h], pointer], axis=1),
                jnp.concatenate([keys, bias], axis=1),
                contract,
                preferred_element_type=f32,
            )

    def slot_rows(kv, h, places):
        return jnp.concatenate([row[kv, b, p, :, pl.ds(h * HD, HD)] for b, p in places], axis=0)

    def slots(places):
        for h, scores in slot_scores(places):
            attend(h, everything, scores, slot_rows(1, h, places), len(places))

    def rows_of(part, bias, first=False):
        for h in range(heads):
            scores = lax.dot_general(q_buf[h], part(0, h), contract, preferred_element_type=f32)
            attend(h, pl.ds(0, rows), scores + bias[...], part(1, h), 4, first)

    near_spread.near[2].wait_recv()
    project(tok_near, 0, 1, True)
    rows_of(lambda kv, h: kv_own[kv, h], bias_own, first=True)
    for copy in z_copies[0, 0] + z_copies[1, 0]:
        copy.wait_recv()
    y_pass(1)
    z_send(1, 1, 2)
    send_straight()
    slots(((0, 0), (0, 1), (0, 2), (1, 0), (2, 0), (3, 0)))

    near_spread.pass_near()
    for back in (1, 3):
        near_spread.near_sibling[back].wait_recv()
        project(tok_near, back, 1, False)
    for copy in y_far[0]:
        copy.wait_recv()
    z_send(0, 3, 1)
    pass_turned()
    near_spread.pass_far()
    for copy in y_far[1]:
        copy.wait_recv()
    z_send(1, 3, 1)
    for copy in near_spread.far_sibling:
        copy.wait_recv()
    project(tok_near, 2, 1, False)
    tok[0] = total[:, : 2 * width].astype(bf16)
    rows_of(lambda kv, h: tok[0, :, pl.ds(kv * width + h * HD, HD)], bias_near)
    for copy in z_copies[0, 1] + z_copies[1, 1]:
        copy.wait_recv()
    slots(((1, 1), (1, 2), (2, 1), (2, 2), (3, 1), (3, 2), (0, 3)))

    for side, copy in far_copies:
        wait_for_side(side, copy)
    for h in range(heads):
        for side in range(2):
            at = halves[side]
            scores = lax.dot_general(q_buf[h, at], kv_far[side, 0, h], contract, preferred_element_type=f32)
            attend(h, at, scores + bias_far[side], kv_far[side, 1, h], 2)

    last_places = ((1, 3), (2, 3), (3, 3))
    span = len(last_places) * BLOCK
    for copy in z_copies[0, 3]:
        copy.wait_recv()
    for h, scores in slot_scores(last_places):
        pieces, keep = weigh(h, everything, scores, len(last_places))
        for i, piece in enumerate(pieces):
            total[:, pl.ds(h * span + i * BLOCK, BLOCK)] = piece
        for side in range(2):
            lanes = pl.ds(side * HD, HD)
            acc_buf[h, :, lanes] = acc_buf[h, :, lanes] * keep
    for copy in z_copies[1, 3]:
        copy.wait_recv()
    out_copies = []
    for h in range(heads):
        pieces = [total[:, pl.ds(h * span + i * BLOCK, BLOCK)] for i in range(len(last_places))]
        sums = acc_buf[h] + mix(pieces, slot_rows(1, h, last_places))
        lanes = pl.ds(h * HD, HD)
        q_buf[h] = (sums[:, :HD] / sums[:, HD:]).astype(out.dtype)
        out_copies.append(pltpu.make_async_copy(q_buf.at[h], out.at[:, lanes], out_sem.at[h]))
        out_copies[h].start()
    for copy in out_copies:
        copy.wait()

    assert len(copies) <= N_COPIES - 3
    for condition, copy in copies:
        if condition is None:
            copy.wait_send()
        else:

            @pl.when(condition)
            def _():
                copy.wait_send()

    for _, _, here, _, onward in turns:

        @pl.when(here)
        def _():
            onward.wait_send()


def body(tokens, w_query, w_key, w_value, cache_keys, cache_values, tile_level, window_map):
    rows, width = tokens.shape
    heads = width // HD
    bf16, f32 = jnp.bfloat16, jnp.float32
    block = (BLOCK, width)
    return pl.pallas_call(
        kernel,
        out_shape=jax.ShapeDtypeStruct((rows, width), bf16),
        in_specs=[pl.BlockSpec(memory_space=pl.ANY)] * 6 + [pl.BlockSpec(memory_space=pltpu.SMEM)] * 2,
        out_specs=pl.BlockSpec(memory_space=pl.ANY),
        scratch_shapes=[
            pltpu.VMEM((4, rows, 2 * width), bf16),
            pltpu.VMEM((4, rows, 2 * width), bf16),
            pltpu.VMEM((4, 2 * width, 3 * width), bf16),
            pltpu.VMEM((rows, 3 * width), f32),
            pltpu.VMEM((heads, rows, HD), bf16),
            pltpu.VMEM((2, heads, rows, HD), bf16),
            pltpu.VMEM((2, 2, heads, rows // 2, HD), bf16),
            pltpu.VMEM((4,) + block, bf16),
            pltpu.VMEM((4, BLOCK, 3 * HD), bf16),
            pltpu.VMEM((4,) + block, bf16),
            pltpu.VMEM((4, BLOCK, 3 * HD), bf16),
            pltpu.VMEM((4, BLOCK, width - 3 * HD), bf16),
            pltpu.VMEM((4, BLOCK, width - 3 * HD), bf16),
            pltpu.VMEM((4,) + block, bf16),
            pltpu.VMEM((4,) + block, bf16),
            pltpu.VMEM((4,) + block, bf16),
            pltpu.VMEM((4,) + block, bf16),
            pltpu.VMEM((2, 3, 4) + block, bf16),
            pltpu.VMEM((2, 4, 4) + block, bf16),
            pltpu.VMEM((heads, rows, HD), f32),
            pltpu.VMEM((heads, rows, 2 * HD), f32),
            pltpu.VMEM((rows, rows), f32),
            pltpu.VMEM((rows, rows), f32),
            pltpu.VMEM((2, rows // 2, rows // 2), f32),
            pltpu.VMEM((8, rows // 2, HD), bf16),
            pltpu.SemaphoreType.DMA((4, 3)),
            pltpu.SemaphoreType.DMA((3,)),
            pltpu.SemaphoreType.DMA((heads,)),
            pltpu.SemaphoreType.DMA((N_COPIES,)),
            pltpu.SemaphoreType.DMA((N_COPIES,)),
        ],
        compiler_params=pltpu.CompilerParams(
            collective_id=0, has_side_effects=True, vmem_limit_bytes=63 * 1024 * 1024
        ),
    )(tokens, w_query, w_key, w_value, cache_keys, cache_values, tile_level, window_map.T)


def solution(mesh):
    placed = (
        P("sp", "tp"),
        P(None, "tp"),
        P(None, "tp"),
        P(None, "tp"),
        P("sp", None, "tp"),
        P("sp", None, "tp"),
        P("sp"),
        P(),
    )
    return jax.shard_map(body, mesh=mesh, in_specs=placed, out_specs=P("sp", "tp"), check_vma=False)
```
